128 devices in a mesh: dp: 2 (over y_lo), ctx: 32 (over z, x, core), branch: 2 (over y_hi).
Axes of the slice: x: 4, y: 4 (y_hi: 2, y_lo: 2; y = y_hi * 2 + y_lo), z: 4, core: 2. Of those that a mesh axis runs over, the one named last changes fastest.
Arguments:
- prompt_query_projection: bfloat16 [2, 4096, 2560], P('dp', ('ctx', 'branch')), may hold values from -16 to 16
- prompt_key_projection: bfloat16 [2, 4096, 512], P('dp', ('ctx', 'branch')), may hold values from -16 to 16
- prompt_value_projection: bfloat16 [2, 4096, 512], P('dp', ('ctx', 'branch')), may hold values from -6 to 6
- prompt_output_gradient: bfloat16 [2, 4096, 2560], P('dp', ('ctx', 'branch')), may hold values from -6 to 6
- response_query: bfloat16 [2, 2, 2048, 2560], P('dp', 'branch', 'ctx'), may hold values from -16 to 16
- response_key_projection: bfloat16 [2, 2, 2048, 512], P('dp', 'branch', 'ctx'), may hold values from -16 to 16
- response_value_projection: bfloat16 [2, 2, 2048, 512], P('dp', 'branch', 'ctx'), may hold values from -6 to 6
- response_output_gradient: bfloat16 [2, 2, 2048, 2560], P('dp', 'branch', 'ctx'), may hold values from -6 to 6
- query_projection_bias: bfloat16 [2560], replicated, may hold values from -3 to 3
- key_projection_bias: bfloat16 [512], replicated, may hold values from -3 to 3
- value_projection_bias: bfloat16 [512], replicated, may hold values from -3 to 3
- segments: int32 [2, 4096], P('dp', ('ctx', 'branch')), may hold values from 0 to 3, never falling along the last dimension, each value on 1 to 2048 neighbouring positions
- lengths: int32 [2, 2], P('dp', 'branch'), may hold values from 512 to 2048, as said below
Outputs:
- prompt_output: bfloat16 [2, 4096, 2560], P('dp', ('ctx', 'branch'))
- response_output: bfloat16 [2, 2, 2048, 2560], P('dp', 'branch', 'ctx')
- prompt_query_grad: bfloat16 [2, 4096, 2560], P('dp', ('ctx', 'branch'))
- prompt_key_grad: bfloat16 [2, 4096, 512], P('dp', ('ctx', 'branch'))
- prompt_value_grad: bfloat16 [2, 4096, 512], P('dp', ('ctx', 'branch'))
- response_query_grad: bfloat16 [2, 2, 2048, 2560], P('dp', 'branch', 'ctx')
- response_key_grad: bfloat16 [2, 2, 2048, 512], P('dp', 'branch', 'ctx')
- response_value_grad: bfloat16 [2, 2, 2048, 512], P('dp', 'branch', 'ctx')
- query_bias_grad: float32 [2560], replicated
- key_bias_grad: float32 [512], replicated
- value_bias_grad: float32 [512], replicated
The draws below stay inside these ranges and needn't reach their ends.
Inputs may be any that keep to these rules, and one draw needn't show every extreme that they name: `segments`: segment ids never fall along the prompt; each segment has at most 2048 positions, and one has exactly that many. In each example one of the two responses has exactly 2048 tokens; a response's tokens are its first lengths positions.
All inputs are finite; a program needn't handle non-finite values.
Results may differ from the reference program's by a relative error of at most 0.025.
The reference program's roundings to bfloat16 on the way count: a program that leaves them out, or rounds other values in their place, can miss the bound.
Values may be sent and summed in bfloat16 or wider, within the bound.
No kernel may reach another device: no remote copies, remote signals or barrier semaphores. Data moves between devices by JAX's collectives and lax.ppermute only.
A program may use at most 128 MiB of HBM per device.

```python
import math
import jax
import jax.numpy as jnp
import numpy as np
from jax import lax

QUERY_HEADS = 20
KEY_VALUE_HEADS = 4
HEAD_SIZE = 128
SEGS = 4
BATCH_EXAMPLES = 2
PROMPT_LENGTH = 4096
RESPONSE_LENGTH = 2048


def align_plan(key, leading_axes, row_number):
    random_subkeys = jax.random.split(key, 5)
    stride = max(row_number // 32, 2)
    offsets = jax.random.randint(random_subkeys[0], (leading_axes, 8), 1, stride)
    places = jnp.arange(8, dtype=jnp.int32)[None, :] * stride + offsets
    preferred_response = jax.random.randint(random_subkeys[1], (leading_axes, 8), 0, KEY_VALUE_HEADS)
    target = jax.random.uniform(random_subkeys[2], (leading_axes, 8), minval=110.0, maxval=360.0)
    spacing = jax.random.uniform(random_subkeys[3], (leading_axes, 8), minval=1.0, maxval=3.0)
    sign_values = jnp.where(jax.random.bernoulli(random_subkeys[4], 0.5, (leading_axes, 8, HEAD_SIZE)), 1.0, -1.0)
    slow_dims = (jnp.arange(HEAD_SIZE) % (HEAD_SIZE // 2) >= HEAD_SIZE // 4).astype(jnp.float32)
    strength = jnp.sqrt(target * HEAD_SIZE ** 0.5 / (HEAD_SIZE // 2))
    vectors = sign_values * slow_dims[None, None, :] * strength[:, :, None]
    row_index = jnp.arange(row_number, dtype=jnp.int32)[None, :, None]
    aligned_rows = (row_index == places[:, None, :]).astype(jnp.float32)
    prior_rows = (row_index == places[:, None, :] - 1).astype(jnp.float32)
    matched_heads = (jnp.arange(KEY_VALUE_HEADS, dtype=jnp.int32)[None, None, :] == preferred_response[:, :, None]).astype(jnp.float32)
    shrink = 1.0 - spacing / target
    return (aligned_rows, prior_rows, matched_heads, vectors, shrink, slow_dims)


def query_field(key, arranged_plan, leading_axes, row_number, quantity, broadcast_heads):
    initial_random_key, second_key = jax.random.split(key)
    aligned_rows, prior_rows, matched_heads, vectors, shrink, slow_dims = arranged_plan
    scaling = jnp.exp(jax.random.uniform(second_key, (leading_axes, row_number, 1, 1, 1), minval=-broadcast_heads, maxval=broadcast_heads))
    backdrop = jnp.clip(jax.random.normal(initial_random_key, (leading_axes, row_number, KEY_VALUE_HEADS, QUERY_HEADS // KEY_VALUE_HEADS, HEAD_SIZE), jnp.float32), -6.0, 6.0)
    backdrop = backdrop * scaling
    selected = jnp.einsum('lrc,lch->lrh', aligned_rows, matched_heads) * quantity
    placed = jnp.einsum('lrc,lch,lcd->lrhd', aligned_rows, matched_heads, vectors)
    return jnp.where(selected[..., None, None] > 0.5, placed[:, :, :, None, :], backdrop)


def key_region(key, arranged_plan, leading_axes, row_number, quantity, broadcast_heads):
    initial_random_key, second_key = jax.random.split(key)
    aligned_rows, prior_rows, matched_heads, vectors, shrink, slow_dims = arranged_plan
    scaling = jnp.exp(jax.random.uniform(second_key, (leading_axes, row_number, 1, 1), minval=-broadcast_heads, maxval=broadcast_heads))
    backdrop = jnp.clip(jax.random.normal(initial_random_key, (leading_axes, row_number, KEY_VALUE_HEADS, HEAD_SIZE), jnp.float32), -6.0, 6.0)
    backdrop = backdrop * scaling
    slow_mask = slow_dims[None, None, None, :] > 0.5
    here_selected = jnp.einsum('lrc,lch->lrh', aligned_rows, matched_heads) * quantity
    here_placed = jnp.einsum('lrc,lch,lcd->lrhd', aligned_rows, matched_heads, vectors)
    prior_selected = jnp.einsum('lrc,lch->lrh', prior_rows, matched_heads) * quantity
    prior_placed = jnp.einsum('lrc,lch,lcd->lrhd', prior_rows, matched_heads, vectors * shrink[:, :, None])
    result = jnp.where((here_selected[..., None] > 0.5) & slow_mask, here_placed, backdrop)
    return jnp.where((prior_selected[..., None] > 0.5) & slow_mask, prior_placed, result)


def draw_prompt_query_projection(key, part):
    arranged_plan = align_plan(jax.random.fold_in(key, 101), BATCH_EXAMPLES, PROMPT_LENGTH)
    key = jax.random.fold_in(key, 1)
    quantity, broadcast_heads = (0.0, 0.0)
    return query_field(key, arranged_plan, BATCH_EXAMPLES, PROMPT_LENGTH, quantity, broadcast_heads).reshape(BATCH_EXAMPLES, PROMPT_LENGTH, QUERY_HEADS * HEAD_SIZE).astype(jnp.bfloat16)


def draw_prompt_key_projection(key, part):
    arranged_plan = align_plan(jax.random.fold_in(key, 101), BATCH_EXAMPLES, PROMPT_LENGTH)
    key = jax.random.fold_in(key, 2)
    quantity, broadcast_heads = (0.0, 0.0)
    return key_region(key, arranged_plan, BATCH_EXAMPLES, PROMPT_LENGTH, quantity, broadcast_heads).reshape(BATCH_EXAMPLES, PROMPT_LENGTH, KEY_VALUE_HEADS * HEAD_SIZE).astype(jnp.bfloat16)


def draw_response_query(key, part):
    arranged_plan = align_plan(jax.random.fold_in(key, 202), BATCH_EXAMPLES * 2, RESPONSE_LENGTH)
    key = jax.random.fold_in(key, 3)
    quantity, broadcast_heads = (0.0, 0.0)
    return query_field(key, arranged_plan, BATCH_EXAMPLES * 2, RESPONSE_LENGTH, quantity, broadcast_heads).reshape(BATCH_EXAMPLES, 2, RESPONSE_LENGTH, QUERY_HEADS * HEAD_SIZE).astype(jnp.bfloat16)


def draw_response_key_projection(key, part):
    arranged_plan = align_plan(jax.random.fold_in(key, 202), BATCH_EXAMPLES * 2, RESPONSE_LENGTH)
    key = jax.random.fold_in(key, 4)
    quantity, broadcast_heads = (0.0, 0.0)
    return key_region(key, arranged_plan, BATCH_EXAMPLES * 2, RESPONSE_LENGTH, quantity, broadcast_heads).reshape(BATCH_EXAMPLES, 2, RESPONSE_LENGTH, KEY_VALUE_HEADS * HEAD_SIZE).astype(jnp.bfloat16)


def draw_lengths(key, part):
    key = jax.random.fold_in(key, 7)
    initial_random_key, second_key = jax.random.split(key)
    longest = jax.random.randint(initial_random_key, (BATCH_EXAMPLES,), 0, 2)
    shorter = jax.random.randint(second_key, (BATCH_EXAMPLES,), RESPONSE_LENGTH // 4, RESPONSE_LENGTH + 1)
    picked = jnp.arange(2, dtype=jnp.int32)[None, :] == longest[:, None]
    return jnp.where(picked, RESPONSE_LENGTH, shorter[:, None]).astype(jnp.int32)


def steps_of(stream_key, shape, cuts, low, largest):
    level, own = 1.0, jax.random.fold_in(stream_key, 6)
    for axis_at, parts in cuts:
        steps = jnp.exp(jax.random.uniform(jax.random.fold_in(own, axis_at), (parts,), jnp.float32, low / len(cuts), largest / len(cuts)))
        level = level * jnp.repeat(steps, shape[axis_at] // parts).reshape([-1 if axis == axis_at else 1 for axis in range(len(shape))])
    return level


def profile(number_of, total, reach, lean):
    portions = [(1 << 20) // math.isqrt(standing ** lean) + 1 for standing in range(2, number_of + 1)]
    spare, holding = total - reach - (number_of - 1), [1] * (number_of - 1)
    while spare > 0:
        free = [i for i in range(number_of - 1) if holding[i] < reach]
        mass, remaining = sum([portions[i] for i in free]), spare
        for i in free:
            addition = min(reach - holding[i], max(1, remaining * portions[i] // mass), spare)
            holding[i] = holding[i] + addition
            spare = spare - addition
    return np.array([reach] + holding)


def ragged(own_key, number_of, total, limit, skew):
    if number_of == 2:
        one = jax.random.randint(own_key, (), max(1, total - limit), min(limit, total - 1) + 1)
        return jnp.stack([one, total - one])
    tallies = jnp.asarray(profile(number_of, total, limit, skew), jnp.int32)
    twos = (number_of - 1) // 2
    giver, taker = tallies[1:1 + 2 * twos:2], tallies[2:2 + 2 * twos:2]
    slack = jnp.minimum(giver - 1, limit - taker)
    moved = jax.random.randint(jax.random.fold_in(own_key, 1), (twos,), 0, 1 << 20) % (slack + 1)
    tallies = tallies.at[1:1 + 2 * twos:2].set(giver - moved).at[2:2 + 2 * twos:2].set(taker + moved)
    return tallies[jax.random.permutation(jax.random.fold_in(own_key, 2), number_of)]


def normal_values(rng, extent, width, reach, cuts=(), held_as=jnp.bfloat16):
    entries = jax.random.normal(rng, extent, jnp.float32) * width
    if len(cuts) > 0:
        entries = steps_of(rng, extent, cuts, -0.22, 0.18) * entries
    return jnp.clip(entries, min=-reach, max=reach).astype(held_as)


def setup_inputs(seed: int = 0) -> dict:
    seeds = jax.random.split(jax.random.key(seed), 14)
    prompt_query_projection = draw_prompt_query_projection(jax.random.fold_in(seeds[13], 71), 0)
    prompt_key_projection = draw_prompt_key_projection(jax.random.fold_in(seeds[13], 71), 0)
    prompt_value_projection = normal_values(seeds[2], (BATCH_EXAMPLES, PROMPT_LENGTH, KEY_VALUE_HEADS * HEAD_SIZE), 1.0, 6.0, ((0, 2), (1, 64)))
    prompt_output_gradient = normal_values(seeds[3], (BATCH_EXAMPLES, PROMPT_LENGTH, QUERY_HEADS * HEAD_SIZE), 1.0, 6.0, ((0, 2), (1, 64)))
    response_query = draw_response_query(jax.random.fold_in(seeds[13], 71), 0)
    response_key_projection = draw_response_key_projection(jax.random.fold_in(seeds[13], 71), 0)
    response_value_projection = normal_values(seeds[6], (BATCH_EXAMPLES, 2, RESPONSE_LENGTH, KEY_VALUE_HEADS * HEAD_SIZE), 1.0, 6.0, ((0, 2), (1, 2), (2, 32)))
    response_output_gradient = normal_values(seeds[7], (BATCH_EXAMPLES, 2, RESPONSE_LENGTH, QUERY_HEADS * HEAD_SIZE), 1.0, 6.0, ((0, 2), (1, 2), (2, 32)))
    query_projection_bias = normal_values(seeds[8], (QUERY_HEADS * HEAD_SIZE,), 0.5, 3.0)
    key_projection_bias = normal_values(seeds[9], (KEY_VALUE_HEADS * HEAD_SIZE,), 0.5, 3.0)
    value_projection_bias = normal_values(seeds[10], (KEY_VALUE_HEADS * HEAD_SIZE,), 0.5, 3.0)
    segments = jax.vmap(lambda own: jnp.searchsorted(jnp.cumsum(ragged(own, SEGS, PROMPT_LENGTH, PROMPT_LENGTH // 2, 0)), jnp.arange(PROMPT_LENGTH), side="right"))(jax.random.split(seeds[11], BATCH_EXAMPLES)).reshape((BATCH_EXAMPLES, PROMPT_LENGTH)).astype(jnp.int32)
    lengths = draw_lengths(jax.random.fold_in(seeds[13], 71), 0)
    return {"prompt_query_projection": prompt_query_projection, "prompt_key_projection": prompt_key_projection, "prompt_value_projection": prompt_value_projection, "prompt_output_gradient": prompt_output_gradient, "response_query": response_query, "response_key_projection": response_key_projection, "response_value_projection": response_value_projection, "response_output_gradient": response_output_gradient, "query_projection_bias": query_projection_bias, "key_projection_bias": key_projection_bias, "value_projection_bias": value_projection_bias, "segments": segments, "lengths": lengths}


rope_base = 1000000.0
score_masked = -1.0e30


def rope_tables(positions, head_dim):
    half_dim = head_dim // 2
    frequency = rope_base ** (-(jnp.arange(half_dim, dtype=jnp.float32) * 2.0 / head_dim))
    angles = positions.astype(jnp.float32)[:, None] * frequency[None, :]
    angles = jnp.concatenate([angles, angles], axis=1)
    return jnp.cos(angles), jnp.sin(angles)


def rotate(values, positions):
    cosine_table, sine_table = rope_tables(positions, values.shape[-1])
    half_dim = values.shape[-1] // 2
    turned = jnp.concatenate([-values[..., half_dim:], values[..., :half_dim]], axis=-1)
    return values * cosine_table[:, None, :] + turned * sine_table[:, None, :]


def inverse_rotation(gradients, positions):
    cosine_table, sine_table = rope_tables(positions, gradients.shape[-1])
    half_dim = gradients.shape[-1] // 2
    scaled = gradients * sine_table[:, None, :]
    turned = jnp.concatenate([scaled[..., half_dim:], -scaled[..., :half_dim]], axis=-1)
    return gradients * cosine_table[:, None, :] + turned


def prepare_inputs(row_values, bias_row, head_count, positions):
    biased = row_values.astype(jnp.float32) + bias_row.astype(jnp.float32)[None, :]
    biased = biased.reshape(row_values.shape[0], head_count, -1)
    return rotate(biased, positions).astype(jnp.bfloat16)


def attend(query_rows_all, incoming_gradient, validity, keys, values, visible_fn):
    query_number = query_rows_all.shape[0]
    block_rows = min(256, query_number)
    blocks = query_number // block_rows
    score_scale = query_rows_all.shape[-1] ** -0.5
    key_wide = keys.astype(jnp.float32)
    value_wide = values.astype(jnp.float32)

    def one_block(carried, block_index):
        key_grad, value_grad = carried
        begin_row = block_index * block_rows
        query_wide = lax.dynamic_slice_in_dim(query_rows_all, begin_row, block_rows, 0).astype(jnp.float32)
        keep_rows = lax.dynamic_slice_in_dim(validity, begin_row, block_rows, 0)
        cot_block = lax.dynamic_slice_in_dim(incoming_gradient, begin_row, block_rows, 0).astype(jnp.float32)
        cot_block = cot_block * keep_rows[:, None, None, None]
        visible = visible_fn(begin_row, block_rows)[None, None]
        scores = jnp.einsum("qgmd,kgd->gmqk", query_wide, key_wide) * score_scale
        scores = jnp.where(visible, scores, score_masked)
        highest = jnp.max(scores, axis=-1, keepdims=True)
        log_total = highest + jnp.log(jnp.sum(jnp.exp(scores - highest), axis=-1, keepdims=True))
        weights = jnp.exp(scores - log_total)
        weights_low = lax.optimization_barrier(weights.astype(jnp.bfloat16)).astype(jnp.float32)
        output = jnp.einsum("gmqk,kgd->qgmd", weights_low, value_wide) * keep_rows[:, None, None, None]
        output_low = output.astype(jnp.bfloat16)
        row_dot = jnp.sum(cot_block * output_low.astype(jnp.float32), axis=-1)
        row_dot = jnp.transpose(row_dot, (1, 2, 0))
        weight_grad = jnp.einsum("qgmd,kgd->gmqk", cot_block, value_wide)
        score_grad = weights * (weight_grad - row_dot[..., None])
        score_low = lax.optimization_barrier(score_grad.astype(jnp.bfloat16)).astype(jnp.float32)
        query_grad = jnp.einsum("gmqk,kgd->qgmd", score_low, key_wide) * score_scale
        key_grad = key_grad + jnp.einsum("gmqk,qgmd->kgd", score_low, query_wide) * score_scale
        value_grad = value_grad + jnp.einsum("gmqk,qgmd->kgd", weights_low, cot_block)
        return (key_grad, value_grad), (output_low, query_grad)

    zeros_start = jnp.zeros(keys.shape, jnp.float32)
    (key_grad, value_grad), (outputs, query_grads) = lax.scan(
        one_block, (zeros_start, zeros_start), jnp.arange(blocks, dtype=jnp.int32))
    outputs = outputs.reshape(query_number, -1)
    query_grads = query_grads.reshape(query_number, -1, query_rows_all.shape[-1])
    return outputs, query_grads, key_grad, value_grad


def reference(prompt_query_projection, prompt_key_projection, prompt_value_projection, prompt_output_gradient, response_query, response_key_projection,
              response_value_projection, response_output_gradient, query_projection_bias, key_projection_bias, value_projection_bias, segments, lengths):
    query_groups = QUERY_HEADS // KEY_VALUE_HEADS
    prompt_slots = jnp.arange(PROMPT_LENGTH, dtype=jnp.int32)
    reply_slots = jnp.arange(RESPONSE_LENGTH, dtype=jnp.int32)
    prompt_outputs, prompt_qgrads, prompt_kgrads, prompt_vgrads = [], [], [], []
    answer_outputs, answer_qgrads, answer_kgrads, answer_vgrads = [], [], [], []
    query_bias_sum = jnp.zeros((QUERY_HEADS * HEAD_SIZE,), jnp.float32)
    key_bias_total = jnp.zeros((KEY_VALUE_HEADS * HEAD_SIZE,), jnp.float32)
    value_bias_total = jnp.zeros((KEY_VALUE_HEADS * HEAD_SIZE,), jnp.float32)
    for example_index in range(BATCH_EXAMPLES):
        segment_ids = segments[example_index]
        query_rows_all = prepare_inputs(prompt_query_projection[example_index], query_projection_bias, QUERY_HEADS, prompt_slots).reshape(PROMPT_LENGTH, KEY_VALUE_HEADS, query_groups, HEAD_SIZE)
        prompt_key_rows = prepare_inputs(prompt_key_projection[example_index], key_projection_bias, KEY_VALUE_HEADS, prompt_slots)
        prompt_values = (prompt_value_projection[example_index].astype(jnp.float32)
                         + value_projection_bias.astype(jnp.float32)[None, :]).astype(jnp.bfloat16).reshape(PROMPT_LENGTH, KEY_VALUE_HEADS, HEAD_SIZE)

        def prompt_visible(begin_row, block_rows):
            query_rows = begin_row + jnp.arange(block_rows, dtype=jnp.int32)
            query_ids = lax.dynamic_slice_in_dim(segment_ids, begin_row, block_rows, 0)
            return (prompt_slots[None, :] <= query_rows[:, None]) & (segment_ids[None, :] == query_ids[:, None])

        prompt_incoming = prompt_output_gradient[example_index].reshape(PROMPT_LENGTH, KEY_VALUE_HEADS, query_groups, HEAD_SIZE)
        outputs, query_grads, key_gradient_total, value_gradient_total = attend(
            query_rows_all, prompt_incoming, jnp.ones((PROMPT_LENGTH,), jnp.float32), prompt_key_rows, prompt_values, prompt_visible)
        prompt_outputs.append(outputs)
        query_pre = inverse_rotation(query_grads.reshape(PROMPT_LENGTH, QUERY_HEADS, HEAD_SIZE), prompt_slots).reshape(PROMPT_LENGTH, QUERY_HEADS * HEAD_SIZE)
        prompt_qgrads.append(query_pre.astype(jnp.bfloat16))
        query_bias_sum = query_bias_sum + jnp.sum(query_pre, axis=0)
        branch_outputs, branch_qgrads, branch_kgrads, branch_vgrads = [], [], [], []
        for response_branch in range(2):
            length = lengths[example_index, response_branch]
            reply_positions = PROMPT_LENGTH + reply_slots
            answer_queries = prepare_inputs(response_query[example_index, response_branch], query_projection_bias, QUERY_HEADS,
                                     reply_positions).reshape(RESPONSE_LENGTH, KEY_VALUE_HEADS, query_groups, HEAD_SIZE)
            reply_keys = prepare_inputs(response_key_projection[example_index, response_branch], key_projection_bias, KEY_VALUE_HEADS, reply_positions)
            answer_values = (response_value_projection[example_index, response_branch].astype(jnp.float32)
                             + value_projection_bias.astype(jnp.float32)[None, :]).astype(jnp.bfloat16).reshape(RESPONSE_LENGTH, KEY_VALUE_HEADS, HEAD_SIZE)
            joined_keys = jnp.concatenate([prompt_key_rows, reply_keys], axis=0)
            joined_values = jnp.concatenate([prompt_values, answer_values], axis=0)

            def answer_visible(begin_row, block_rows):
                query_rows = begin_row + jnp.arange(block_rows, dtype=jnp.int32)
                later = (reply_slots[None, :] <= query_rows[:, None]) & (reply_slots[None, :] < length)
                return jnp.concatenate([jnp.ones((block_rows, PROMPT_LENGTH), bool), later], axis=1)

            validity = (reply_slots < length).astype(jnp.float32)
            reply_cotangent = response_output_gradient[example_index, response_branch].reshape(RESPONSE_LENGTH, KEY_VALUE_HEADS, query_groups, HEAD_SIZE)
            outputs, query_grads, key_gradients, value_gradients = attend(
                answer_queries, reply_cotangent, validity, joined_keys, joined_values, answer_visible)
            key_gradient_total = key_gradient_total + key_gradients[:PROMPT_LENGTH]
            value_gradient_total = value_gradient_total + value_gradients[:PROMPT_LENGTH]
            branch_outputs.append(outputs)
            query_pre = inverse_rotation(query_grads.reshape(RESPONSE_LENGTH, QUERY_HEADS, HEAD_SIZE), reply_positions).reshape(RESPONSE_LENGTH, QUERY_HEADS * HEAD_SIZE)
            key_unbiased = inverse_rotation(key_gradients[PROMPT_LENGTH:], reply_positions).reshape(RESPONSE_LENGTH, KEY_VALUE_HEADS * HEAD_SIZE)
            value_unbiased = value_gradients[PROMPT_LENGTH:].reshape(RESPONSE_LENGTH, KEY_VALUE_HEADS * HEAD_SIZE)
            branch_qgrads.append(query_pre.astype(jnp.bfloat16))
            branch_kgrads.append(key_unbiased.astype(jnp.bfloat16))
            branch_vgrads.append(value_unbiased.astype(jnp.bfloat16))
            query_bias_sum = query_bias_sum + jnp.sum(query_pre, axis=0)
            key_bias_total = key_bias_total + jnp.sum(key_unbiased, axis=0)
            value_bias_total = value_bias_total + jnp.sum(value_unbiased, axis=0)
        key_unbiased = inverse_rotation(key_gradient_total, prompt_slots).reshape(PROMPT_LENGTH, KEY_VALUE_HEADS * HEAD_SIZE)
        value_unbiased = value_gradient_total.reshape(PROMPT_LENGTH, KEY_VALUE_HEADS * HEAD_SIZE)
        prompt_kgrads.append(key_unbiased.astype(jnp.bfloat16))
        prompt_vgrads.append(value_unbiased.astype(jnp.bfloat16))
        key_bias_total = key_bias_total + jnp.sum(key_unbiased, axis=0)
        value_bias_total = value_bias_total + jnp.sum(value_unbiased, axis=0)
        answer_outputs.append(jnp.stack(branch_outputs))
        answer_qgrads.append(jnp.stack(branch_qgrads))
        answer_kgrads.append(jnp.stack(branch_kgrads))
        answer_vgrads.append(jnp.stack(branch_vgrads))
    return (jnp.stack(prompt_outputs), jnp.stack(answer_outputs), jnp.stack(prompt_qgrads),
            jnp.stack(prompt_kgrads), jnp.stack(prompt_vgrads), jnp.stack(answer_qgrads),
            jnp.stack(answer_kgrads), jnp.stack(answer_vgrads), query_bias_sum, key_bias_total, value_bias_total)
```

```python
import functools

import jax
import jax.numpy as jnp
import numpy as np
from jax import lax
from jax.experimental import pallas as pl
from jax.experimental.pallas import tpu as pltpu
from jax.sharding import Mesh
from jax.sharding import PartitionSpec as P

HEADS = 4
GROUP = 5
HD = 128
ROWS = 64
STRIPE = GROUP * ROWS
PROMPT = 4096
REPLY = 2048
BLOCK = 512
SCALE = HD**-0.5
LOG2 = float(SCALE * np.log2(np.e))
LOW = -1e30
MASKED = -3e38
KV = 2 * ROWS
PKV = KV + 16
OWN = PKV + KV
PIECE = 4 * OWN + 4 * PKV

bf16 = jnp.bfloat16
f32 = jnp.float32
NT = (((1,), (1,)), ((), ()))
NN = (((1,), (0,)), ((), ()))
TN = (((0,), (0,)), ((), ()))


def dot(a, b, dims):
    return lax.dot_general(a, b, dims, preferred_element_type=f32)


def angle_tables():
    frequency = 1000000.0 ** (-(np.arange(HD // 2) * 2.0 / HD))
    frequency = np.concatenate([frequency, frequency])
    sign = np.where(np.arange(HD) < HD // 2, -1.0, 1.0)
    coarse = np.arange((PROMPT + REPLY) // ROWS)[:, None] * ROWS * frequency
    fine = np.arange(ROWS)[:, None] * frequency
    return [
        jnp.asarray(t.astype(np.float32))
        for t in (np.cos(coarse), np.sin(coarse) * sign, np.cos(fine), np.sin(fine) * sign)
    ]


def turn(tables, block):
    coarse_cos, coarse_sin, fine_cos, fine_sin = tables
    ca, sa = coarse_cos[pl.ds(block, 1), :], coarse_sin[pl.ds(block, 1), :]
    cb, sb = fine_cos[...], fine_sin[...]
    return ca * cb - sa * sb, sa * cb + ca * sb


def rotate(x, cosine, sine):
    return x * cosine + pltpu.roll(x, HD // 2, 1) * sine


def unrotate(x, cosine, sine):
    return x * cosine - pltpu.roll(x, HD // 2, 1) * sine


def prompt_block(sc, z):
    return z * 16 + sc[1] * 4 + sc[2] * 2 + sc[3]


def reply_block(sc, z):
    return z * 8 + sc[1] * 2 + sc[2]


def part(i):
    return pl.ds(pl.multiple_of(i, ROWS), ROWS)


def lanes(i):
    return pl.ds(pl.multiple_of(i * HD, HD), HD)


def prepare_kv_body(sc, pk, pv, rk, rv, kbias, vbias, seg, t0, t1, t2, t3, *outs):
    tables = (t0, t1, t2, t3)
    z = sc[0]
    prompt_turn = turn(tables, prompt_block(sc, z))
    reply_turn = turn(tables, PROMPT // ROWS + reply_block(sc, z))
    ids = seg[...]
    row = lax.broadcasted_iota(jnp.int32, (16, HD), 0)
    lane = lax.broadcasted_iota(jnp.int32, (16, HD), 1)
    note = jnp.zeros((16, HD), f32)
    for s in range(1, HEADS):
        below = jnp.sum((ids < s).astype(f32), axis=1, keepdims=True) * 0.5
        note = jnp.where((row == 0) & (lane == s), below, note)
    note = jnp.where(row == 1, ids.astype(f32), note).astype(bf16)
    for s, out in enumerate(outs):
        at = lanes(lax.rem(z + s, HEADS))
        kb, vb = kbias[:, at].astype(f32), vbias[:, at].astype(f32)
        out[0:64, :] = rotate(pk[:, at].astype(f32) + kb, *prompt_turn).astype(bf16)
        out[64:128, :] = (pv[:, at].astype(f32) + vb).astype(bf16)
        out[128:144, :] = note
        out[144:208, :] = rotate(rk[:, at].astype(f32) + kb, *reply_turn).astype(bf16)
        out[208:272, :] = (rv[:, at].astype(f32) + vb).astype(bf16)


def prepare_q_body(sc, pq, pg, rq, rg, qbias, t0, t1, t2, t3, *outs):
    tables = (t0, t1, t2, t3)
    z = sc[0]
    prompt_turn = turn(tables, prompt_block(sc, z))
    reply_turn = turn(tables, PROMPT // ROWS + reply_block(sc, z))
    place = reply_block(sc, z) * ROWS + lax.broadcasted_iota(jnp.int32, (ROWS, HD), 0)
    valid = place < sc[4]
    for s, out in enumerate(outs):
        h = lax.rem(z + s, HEADS) * GROUP
        for m in range(GROUP):
            at = lanes(h + m)
            qb = qbias[:, at].astype(f32)
            o = m * ROWS
            out[o : o + 64, :] = rotate(pq[:, at].astype(f32) + qb, *prompt_turn).astype(bf16)
            o += STRIPE
            out[o : o + 64, :] = pg[:, at]
            o += STRIPE
            out[o : o + 64, :] = rotate(rq[:, at].astype(f32) + qb, *reply_turn).astype(bf16)
            o += STRIPE
            out[o : o + 64, :] = jnp.where(valid, rg[:, at].astype(f32), 0.0).astype(bf16)


def attend_body(
    sc, *refs
):
    q_in, kv_in, tables = refs[0:4], refs[4:12], refs[12:16]
    o_out, dq_out, send, keep, bias_out = refs[16:20], refs[20:24], refs[24:28], refs[28:32], refs[32]
    (pq, pg, rq, rg, pk, pv, rk, rv, pdq, rdq, pdk, pdv, rdk, rdv, p_lse, p_rd, stat_m, stat_l,
     acc_r, note) = refs[33:]
    z, x, core, b, length = sc[0], sc[1], sc[2], sc[3], sc[4]

    for s in range(4):
        at = pl.ds(pl.multiple_of(lax.rem(z + 4 - s, 4) * STRIPE, STRIPE), STRIPE)
        for i, ref in enumerate((pq, pg, rq, rg)):
            ref[at, :] = q_in[s][i * STRIPE : (i + 1) * STRIPE, :]
    counts = jnp.zeros((16, HD), f32)
    for s in range(4):
        xx = lax.rem(x + 4 - s, 4)
        for other in range(2):
            piece = kv_in[s * 2 + other]
            cc = core if other == 0 else 1 - core
            for t in range(4):
                zz = lax.rem(z + 4 - t, 4)
                to = part((zz * 8 + xx * 2 + cc) * ROWS)
                o = t * OWN + PKV
                rk[to, :] = piece[o : o + 64, :]
                rv[to, :] = piece[o + 64 : o + 128, :]
                for far in range(2):
                    bb = b if far == 0 else 1 - b
                    to = part((zz * 16 + xx * 4 + cc * 2 + bb) * ROWS)
                    o = t * OWN if far == 0 else 4 * OWN + t * PKV
                    pk[to, :] = piece[o : o + 64, :]
                    pv[to, :] = piece[o + 64 : o + 128, :]
                    told = piece[o + 128 : o + 144, :].astype(f32)
                    counts = counts + told
                    if s == 0 and other == 0 and far == 0:
                        note[pl.ds(zz, 1)] = told[None]

    lane = lax.broadcasted_iota(jnp.int32, (1, HD), 1)
    starts = [
        jnp.sum(jnp.where(lane == s, counts[0:1, :], 0.0)).astype(jnp.int32) for s in range(HEADS)
    ]

    def prompt_limits(j):
        ids = note[j, 1:2, :].astype(jnp.int32)
        start = jnp.zeros((1, HD), jnp.int32)
        for s in range(1, HEADS):
            start = jnp.where(ids == s, starts[s], start)
        first = jnp.sum(jnp.where(lane == 0, start, 0))
        place = prompt_block(sc, j) * ROWS + jnp.bitwise_and(lane, ROWS - 1)
        start = jnp.concatenate([start, start, start[:, :64]], axis=1)
        place = jnp.concatenate([place, place, place[:, :64]], axis=1)
        lowest = first // BLOCK
        highest = (prompt_block(sc, j) * ROWS + ROWS - 1) // BLOCK + 1
        return start, place, lowest, highest

    def prompt_seen(key_at, start, place):
        key = key_at + lax.broadcasted_iota(jnp.int32, (BLOCK, STRIPE), 0)
        return (key >= start) & (key <= place)

    column = lax.broadcasted_iota(jnp.int32, (1, 4 * STRIPE), 1)
    stripe = sum((column >= j * STRIPE).astype(jnp.int32) for j in range(1, 4))
    reply_place = reply_block(sc, stripe) * ROWS + jnp.bitwise_and(column, ROWS - 1)

    def reply_seen(key_at, place):
        key = key_at + lax.broadcasted_iota(jnp.int32, (BLOCK, place.shape[1]), 0)
        return (key < length) & (key <= place)

    def online(state, q, k, v, seen):
        top, total, acc = state
        scores = dot(k, q, NT) * LOG2
        if seen is not None:
            scores = jnp.where(seen, scores, MASKED)
        raised = jnp.maximum(top, jnp.max(scores, axis=0, keepdims=True))
        shrink = jnp.exp2(top - raised)
        p = jnp.exp2(scores - raised)
        total = total * shrink + jnp.sum(p, axis=0, keepdims=True)
        return raised, total, acc * shrink + dot(v, p.astype(bf16), TN)

    def empty(n):
        return jnp.full((1, n), LOW, f32), jnp.zeros((1, n), f32), jnp.zeros((HD, n), f32)

    q_all = rq[...]

    def forward_reply(i, state):
        at = pl.ds(pl.multiple_of(i * BLOCK, BLOCK), BLOCK)
        return online(state, q_all, pk[at, :], pv[at, :], None)

    top, total, acc = lax.fori_loop(0, PROMPT // BLOCK, forward_reply, empty(4 * STRIPE))
    half = 2 * STRIPE
    for i in range(4):
        at = slice(i * BLOCK, (i + 1) * BLOCK)
        if i < 2:
            top, total, acc = online(
                (top, total, acc), q_all, rk[at, :], rv[at, :], reply_seen(i * BLOCK, reply_place)
            )
            if i == 1:
                stat_m[0:1, :] = top
                stat_l[0:1, :] = total
                acc_r[...] = acc
                state = (top[:, half:], total[:, half:], acc[:, half:])
        else:
            state = online(
                state, rq[half:, :], rk[at, :], rv[at, :], reply_seen(i * BLOCK, reply_place[:, half:])
            )
    stat_m[0:1, half:] = state[0]
    stat_l[0:1, half:] = state[1]
    acc_r[:, half:] = state[2]
    total = stat_l[0:1, :]
    r_lse = stat_m[0:1, :] + jnp.log2(total)
    out = jnp.where(reply_place < length, acc_r[...] / total, 0.0).astype(bf16).astype(f32)
    r_rd = jnp.sum(out * rg[...].astype(f32).T, axis=0, keepdims=True)
    stat_m[0:1, :] = r_lse
    stat_l[0:1, :] = r_rd
    acc_r[...] = out
    out = acc_r[...].T.astype(bf16)
    rk_out = out

    p_out = []
    limits = [prompt_limits(j) for j in range(4)]
    for j in range(4):
        start, place, lowest, highest = limits[j]
        rows = slice(j * STRIPE, (j + 1) * STRIPE)

        def forward_prompt(i, state, rows=rows, start=start, place=place):
            key_at = pl.multiple_of(i * BLOCK, BLOCK)
            at = pl.ds(key_at, BLOCK)
            return online(
                state, pq[rows, :], pk[at, :], pv[at, :], prompt_seen(key_at, start, place)
            )

        top, total, acc = lax.fori_loop(lowest, highest, forward_prompt, empty(STRIPE))
        out = (acc / total).astype(bf16).astype(f32)
        p_lse[j, 0:1, :] = top + jnp.log2(total)
        p_rd[j, 0:1, :] = jnp.sum(out * pg[rows, :].astype(f32).T, axis=0, keepdims=True)
        p_out.append(out.T.astype(bf16))
    pdq[...] = jnp.concatenate(p_out, axis=0).astype(f32)
    rdq[...] = rk_out.astype(f32)
    for s in range(4):
        at = pl.ds(pl.multiple_of(lax.rem(z + 4 - s, 4) * STRIPE, STRIPE), STRIPE)
        o_out[s][0:STRIPE, :] = pdq[at, :].astype(bf16)
        o_out[s][STRIPE:, :] = rdq[at, :].astype(bf16)

    pdq[...] = jnp.zeros_like(pdq)
    rdq[...] = jnp.zeros_like(rdq)

    def grads(q, g, lse, rd, k, v, seen):
        w = jnp.exp2(dot(k, q, NT) * LOG2 - lse)
        if seen is not None:
            w = jnp.where(seen, w, 0.0)
        ds = (w * (dot(v, g, NT) - rd)).astype(bf16)
        return dot(ds, q, NN), dot(w.astype(bf16), g, NN), dot(ds, k, TN)

    def backward_reply(i, carry):
        at = pl.ds(pl.multiple_of(i * BLOCK, BLOCK), BLOCK)
        dk, dv, dq = grads(
            rq[...], rg[...], stat_m[0:1, :], stat_l[0:1, :], pk[at, :], pv[at, :], None
        )
        pdk[at, :] = dk
        pdv[at, :] = dv
        rdq[...] += dq
        return carry

    lax.fori_loop(0, PROMPT // BLOCK, backward_reply, 0)
    for j in range(4):
        start, place, lowest, highest = limits[j]
        rows = slice(j * STRIPE, (j + 1) * STRIPE)

        def backward_prompt(i, carry, j=j, rows=rows, start=start, place=place):
            key_at = pl.multiple_of(i * BLOCK, BLOCK)
            at = pl.ds(key_at, BLOCK)
            dk, dv, dq = grads(
                pq[rows, :], pg[rows, :], p_lse[j, 0:1, :], p_rd[j, 0:1, :],
                pk[at, :], pv[at, :], prompt_seen(key_at, start, place),
            )
            pdk[at, :] += dk
            pdv[at, :] += dv
            pdq[rows, :] += dq
            return carry

        lax.fori_loop(lowest, highest, backward_prompt, 0)
    for i in range(4):
        at = slice(i * BLOCK, (i + 1) * BLOCK)
        cols = slice(0 if i < 2 else half, 4 * STRIPE)
        dk, dv, dq = grads(
            rq[cols, :], rg[cols, :], stat_m[0:1, cols], stat_l[0:1, cols], rk[at, :], rv[at, :],
            reply_seen(i * BLOCK, reply_place[:, cols]),
        )
        rdk[at, :] = dk
        rdv[at, :] = dv
        rdq[cols, :] += dq

    head_sums = [jnp.zeros((1, HD), f32) for _ in range(GROUP)]
    for s in range(4):
        zz = lax.rem(z + 4 - s, 4)
        for i, (ref, base) in enumerate(
            ((pdq, prompt_block(sc, zz)), (rdq, PROMPT // ROWS + reply_block(sc, zz)))
        ):
            cosine, sine = turn(tables, base)
            for m in range(GROUP):
                at = part(zz * STRIPE + m * ROWS)
                pre = unrotate(ref[at, :] * SCALE, cosine, sine)
                head_sums[m] = head_sums[m] + jnp.sum(pre, axis=0, keepdims=True)
                o = i * STRIPE + m * ROWS
                dq_out[s][o : o + ROWS, :] = pre.astype(bf16)

    def sum_rows(i, carry):
        key_sum, value_sum = carry
        at = part(i * ROWS)
        cosine, sine = turn(tables, i)
        return key_sum + unrotate(pdk[at, :], cosine, sine), value_sum + pdv[at, :]

    def sum_reply_rows(i, carry):
        key_sum, value_sum = carry
        at = part(i * ROWS)
        cosine, sine = turn(tables, PROMPT // ROWS + i)
        return key_sum + unrotate(rdk[at, :], cosine, sine), value_sum + rdv[at, :]

    zero = jnp.zeros((ROWS, HD), f32)
    sums = lax.fori_loop(0, PROMPT // ROWS, sum_rows, (zero, zero))
    key_sum, value_sum = lax.fori_loop(0, REPLY // ROWS, sum_reply_rows, sums)
    for m in range(GROUP):
        bias_out[m : m + 1, :] = head_sums[m]
    bias_out[5:6, :] = jnp.sum(key_sum, axis=0, keepdims=True) * SCALE
    bias_out[6:7, :] = jnp.sum(value_sum, axis=0, keepdims=True)
    bias_out[7:8, :] = jnp.zeros((1, HD), f32)
    for s in range(4):
        xx = lax.rem(x + s, 4)
        for t in range(4):
            zz = lax.rem(z + t, 4)
            for far in range(2):
                bb = b if far == 0 else 1 - b
                own = part((zz * 16 + xx * 4 + core * 2 + bb) * ROWS)
                theirs = part((zz * 16 + xx * 4 + (1 - core) * 2 + bb) * ROWS)
                o = far * 512 + t * ROWS
                keep[s][o : o + 64, :] = pdk[own, :] * SCALE
                keep[s][o + 256 : o + 320, :] = pdv[own, :]
                send[s][o : o + 64, :] = (pdk[theirs, :] * SCALE).astype(bf16)
                send[s][o + 256 : o + 320, :] = pdv[theirs, :].astype(bf16)
            own = part((zz * 8 + xx * 2 + core) * ROWS)
            theirs = part((zz * 8 + xx * 2 + 1 - core) * ROWS)
            o = 1024 + t * ROWS
            keep[s][o : o + 64, :] = rdk[own, :] * SCALE
            keep[s][o + 256 : o + 320, :] = rdv[own, :]
            send[s][o : o + 64, :] = (rdk[theirs, :] * SCALE).astype(bf16)
            send[s][o + 256 : o + 320, :] = rdv[theirs, :].astype(bf16)


def settle_body(sc, total, far, t0, t1, t2, t3, *outs):
    tables = (t0, t1, t2, t3)
    z = sc[0]
    for t, out in enumerate(outs):
        zz = lax.rem(z + t, 4)
        o = t * ROWS
        key = total[o : o + 64, :] + far[o : o + 64, :].astype(f32)
        out[0:64, :] = unrotate(key, *turn(tables, prompt_block(sc, zz))).astype(bf16)
        value = total[o + 256 : o + 320, :] + far[o + 256 : o + 320, :].astype(f32)
        out[64:128, :] = value.astype(bf16)
        o += 1024
        base = PROMPT // ROWS + reply_block(sc, zz)
        out[128:192, :] = unrotate(total[o : o + 64, :], *turn(tables, base)).astype(bf16)
        out[192:256, :] = total[o + 256 : o + 320, :].astype(bf16)


def gather_heads_body(step, sc, *refs):
    pieces, outs = refs[:4], refs[4:]
    z = sc[0]
    for s, piece in enumerate(pieces):
        h = lax.rem(z + (s * step) % 4, 4)
        width = piece.shape[0] // ROWS // len(outs)
        for i, out in enumerate(outs):
            for m in range(width):
                o = (i * width + m) * ROWS
                out[:, lanes(h * width + m)] = piece[o : o + ROWS, :]


def call(body, n_in, outs, scratch=()):
    spec = pl.BlockSpec(memory_space=pltpu.VMEM)
    return pl.pallas_call(
        body,
        in_specs=[pl.BlockSpec(memory_space=pltpu.SMEM)] + [spec] * n_in,
        out_specs=[spec] * len(outs),
        out_shape=[jax.ShapeDtypeStruct(s, t) for s, t in outs],
        scratch_shapes=list(scratch),
        compiler_params=pltpu.CompilerParams(vmem_limit_bytes=56 * 1024 * 1024),
    )


def shift(v, axis, s):
    n = lax.axis_size(axis)
    return lax.ppermute(v, axis, [(i, (i + s) % n) for i in range(n)])


def swap(v, axis, bit):
    return lax.ppermute(v, axis, [(i, i ^ bit) for i in range(lax.axis_size(axis))])


def on_device(pq, pk, pv, pg, rq, rk, rv, rg, qbias, kbias, vbias, segments, lengths):
    sc = jnp.stack(
        [lax.axis_index(a) for a in ("z", "x", "core", "branch")] + [lengths[0, 0]]
    ).astype(jnp.int32)
    tables = angle_tables()
    kbias, vbias, qbias = kbias[None], vbias[None], qbias[None]
    seg = jnp.concatenate([segments, segments], axis=1)
    kv = call(prepare_kv_body, 11, [((OWN, HD), bf16)] * 4)(
        sc, pk[0], pv[0], rk[0, 0], rv[0, 0], kbias, vbias, seg, *tables
    )
    kv = jnp.stack([kv[0]] + [shift(kv[s], "z", s) for s in (1, 2, 3)])
    q = call(prepare_q_body, 9, [((4 * STRIPE, HD), bf16)] * 4)(
        sc, pq[0], pg[0], rq[0, 0], rg[0, 0], qbias, *tables
    )
    q = [q[0]] + [shift(q[s], "z", s) for s in (1, 2, 3)]
    far = shift(kv[:, :PKV].reshape(4 * PKV, HD), "branch", 1)
    kv = jnp.concatenate([kv.reshape(4 * OWN, HD), far])
    pieces = []
    for s in range(4):
        piece = kv if s == 0 else shift(kv, "x", s)
        pieces += [piece, shift(piece, "core", 1)]

    rows = 4 * STRIPE
    outs = call(
        attend_body,
        16,
        [((2 * STRIPE, HD), bf16)] * 8 + [((1536, HD), bf16)] * 4 + [((1536, HD), f32)] * 4
        + [((8, HD), f32)],
        [pltpu.VMEM((rows, HD), bf16)] * 4
        + [pltpu.VMEM((PROMPT, HD), bf16)] * 2
        + [pltpu.VMEM((REPLY, HD), bf16)] * 2
        + [pltpu.VMEM((rows, HD), f32)] * 2
        + [pltpu.VMEM((PROMPT, HD), f32)] * 2
        + [pltpu.VMEM((REPLY, HD), f32)] * 2
        + [pltpu.VMEM((4, 8, STRIPE), f32)] * 2
        + [pltpu.VMEM((8, rows), f32)] * 2
        + [pltpu.VMEM((HD, rows), f32), pltpu.VMEM((4, 16, HD), f32)],
    )(sc, *q, *pieces, *tables)
    o, dq, send, keep, bias = outs[0:4], outs[4:8], outs[8:12], outs[12:16], outs[16]

    o = [o[0]] + [shift(o[s], "z", -s) for s in (1, 2, 3)]
    dq = [dq[0]] + [shift(dq[s], "z", -s) for s in (1, 2, 3)]
    summed = [keep[s] + shift(send[s], "core", 1).astype(f32) for s in range(4)]
    total = summed[0]
    for s in (1, 2, 3):
        total = total + shift(summed[s].astype(bf16), "x", s).astype(f32)
    near = shift(total[512:1024].astype(bf16), "branch", 1)
    dkv = call(settle_body, 6, [((4 * ROWS, HD), bf16)] * 4)(sc, total, near, *tables)
    dkv = [dkv[0]] + [shift(dkv[s], "z", s) for s in (1, 2, 3)]

    wide = ((ROWS, HEADS * GROUP * HD), bf16)
    narrow = ((ROWS, HEADS * HD), bf16)
    p_out, r_out = call(functools.partial(gather_heads_body, 1), 4, [wide] * 2)(sc, *o)
    p_dq, r_dq = call(functools.partial(gather_heads_body, 1), 4, [wide] * 2)(sc, *dq)
    p_dk, p_dv, r_dk, r_dv = call(functools.partial(gather_heads_body, 3), 4, [narrow] * 4)(
        sc, *dkv
    )

    bias = bias + swap(bias, "core", 1)
    bias = bias + swap(bias, "x", 1)
    bias = bias + swap(bias, "x", 2)
    bias = bias + swap(bias, "branch", 1)
    bias = bias + swap(bias, "dp", 1)
    z = lax.axis_index("z")
    bias = jnp.where(jnp.arange(4)[:, None, None] == z, bias[None], 0.0)
    bias = bias + swap(bias, "z", 1)
    bias = bias + swap(bias, "z", 2)
    return (
        p_out[None],
        r_out[None, None],
        p_dq[None],
        p_dk[None],
        p_dv[None],
        r_dq[None, None],
        r_dk[None, None],
        r_dv[None, None],
        bias[:, :5].reshape(-1),
        bias[:, 5].reshape(-1),
        bias[:, 6].reshape(-1),
    )


def solution(mesh):
    fine = Mesh(mesh.devices.reshape(2, 4, 4, 2, 2), ("dp", "z", "x", "core", "branch"))
    prompt = P("dp", ("z", "x", "core", "branch"), None)
    reply = P("dp", "branch", ("z", "x", "core"), None)
    return jax.shard_map(
        on_device,
        mesh=fine,
        in_specs=(prompt,) * 4
        + (reply,) * 4
        + (P(),) * 3
        + (P("dp", ("z", "x", "core", "branch")), P("dp", "branch")),
        out_specs=(prompt, reply, prompt, prompt, prompt, reply, reply, reply, P(), P(), P()),
        check_vma=False,
    )
```

```python
import functools

import jax
import jax.numpy as jnp
import numpy as np
from jax import lax
from jax.experimental import pallas as pl
from jax.experimental.pallas import tpu as pltpu
from jax.sharding import Mesh
from jax.sharding import PartitionSpec as P

HEADS = 4
GROUP = 5
HD = 128
ROWS = 64
STRIPE = GROUP * ROWS
PROMPT = 4096
REPLY = 2048
BLOCK = 512
SCALE = HD**-0.5
LOG2 = float(SCALE * np.log2(np.e))
LOW = -1e30
MASKED = -3e38
KV = 2 * ROWS
PKV = KV + 16
OWN = PKV + KV
PIECE = 4 * OWN + 4 * PKV
TERMS = 1536

bf16 = jnp.bfloat16
f32 = jnp.float32
NT = (((1,), (1,)), ((), ()))
NN = (((1,), (0,)), ((), ()))
TN = (((0,), (0,)), ((), ()))


def dot(a, b, dims):
    return lax.dot_general(a, b, dims, preferred_element_type=f32)


def angle_tables():
    frequency = 1000000.0 ** (-(np.arange(HD // 2) * 2.0 / HD))
    frequency = np.concatenate([frequency, frequency])
    sign = np.where(np.arange(HD) < HD // 2, -1.0, 1.0)
    coarse = np.arange((PROMPT + REPLY) // ROWS)[:, None] * ROWS * frequency
    fine = np.arange(ROWS)[:, None] * frequency
    return [
        jnp.asarray(t.astype(np.float32))
        for t in (np.cos(coarse), np.sin(coarse) * sign, np.cos(fine), np.sin(fine) * sign)
    ]


def turn(tables, block):
    coarse_cos, coarse_sin, fine_cos, fine_sin = tables
    ca, sa = coarse_cos[pl.ds(block, 1), :], coarse_sin[pl.ds(block, 1), :]
    cb, sb = fine_cos[...], fine_sin[...]
    return ca * cb - sa * sb, sa * cb + ca * sb


def rotate(x, cosine, sine):
    return x * cosine + pltpu.roll(x, HD // 2, 1) * sine


def unrotate(x, cosine, sine):
    return x * cosine - pltpu.roll(x, HD // 2, 1) * sine


def prompt_block(sc, z):
    return z * 16 + sc[1] * 4 + sc[2] * 2 + sc[3]


def reply_block(sc, z):
    return z * 8 + sc[1] * 2 + sc[2]


def part(i):
    return pl.ds(pl.multiple_of(i, ROWS), ROWS)


def lanes(i):
    return pl.ds(pl.multiple_of(i * HD, HD), HD)


def prepare_kv_body(sc, pk, pv, rk, rv, bias, seg, t0, t1, t2, t3, *outs):
    tables = (t0, t1, t2, t3)
    z = sc[0]
    prompt_turn = turn(tables, prompt_block(sc, z))
    reply_turn = turn(tables, PROMPT // ROWS + reply_block(sc, z))
    ids = jnp.concatenate([seg[...], seg[...]], axis=1)
    row = lax.broadcasted_iota(jnp.int32, (16, HD), 0)
    lane = lax.broadcasted_iota(jnp.int32, (16, HD), 1)
    note = jnp.zeros((16, HD), f32)
    for s in range(1, HEADS):
        below = jnp.sum((ids < s).astype(f32), axis=1, keepdims=True) * 0.5
        note = jnp.where((row == 0) & (lane == s), below, note)
    note = jnp.where(row == 1, ids.astype(f32), note).astype(bf16)
    for s, out in enumerate(outs):
        h = lax.rem(z + s, HEADS)
        at = lanes(h)
        kb, vb = bias[:, lanes(20 + h)].astype(f32), bias[:, lanes(24 + h)].astype(f32)
        out[0:64, :] = rotate(pk[:, at].astype(f32) + kb, *prompt_turn).astype(bf16)
        out[64:128, :] = (pv[:, at].astype(f32) + vb).astype(bf16)
        out[128:144, :] = note
        out[144:208, :] = rotate(rk[:, at].astype(f32) + kb, *reply_turn).astype(bf16)
        out[208:272, :] = (rv[:, at].astype(f32) + vb).astype(bf16)


def prepare_q_body(sc, pq, pg, rq, rg, bias, t0, t1, t2, t3, *outs):
    tables = (t0, t1, t2, t3)
    z = sc[0]
    prompt_turn = turn(tables, prompt_block(sc, z))
    reply_turn = turn(tables, PROMPT // ROWS + reply_block(sc, z))
    place = reply_block(sc, z) * ROWS + lax.broadcasted_iota(jnp.int32, (ROWS, HD), 0)
    valid = place < sc[4]
    for s, out in enumerate(outs):
        h = lax.rem(z + s, HEADS) * GROUP
        for m in range(GROUP):
            at = lanes(h + m)
            qb = bias[:, at].astype(f32)
            o = m * ROWS
            out[o : o + 64, :] = rotate(pq[:, at].astype(f32) + qb, *prompt_turn).astype(bf16)
            o += STRIPE
            out[o : o + 64, :] = pg[:, at]
            o += STRIPE
            out[o : o + 64, :] = rotate(rq[:, at].astype(f32) + qb, *reply_turn).astype(bf16)
            o += STRIPE
            out[o : o + 64, :] = jnp.where(valid, rg[:, at].astype(f32), 0.0).astype(bf16)


def granule(s, zz, sub=0):
    return s * 1024 + zz * 256 + sub * ROWS


def x_of(sc, s):
    return lax.rem(sc[1] + 4 - s, 4)


def prompt_rows(sc, i):
    pair = [granule(lax.rem(sc[1] + 4 - lax.rem(i, 2) * 2 - n, 4), i // 2) for n in range(2)]
    return [pl.ds(pl.multiple_of(row, 256), 256) for row in pair]


def prompt_block_of(sc, i, count, pk, pv, start, place):
    rows = prompt_rows(sc, jnp.minimum(i, PROMPT // BLOCK - 1))
    key = i * BLOCK + lax.broadcasted_iota(jnp.int32, (BLOCK, STRIPE), 0)
    k, v = [jnp.concatenate([ref[at, :] for at in rows], axis=0) for ref in (pk, pv)]
    return k, v, (key >= start) & (key <= jnp.where(i < count, place, -1))


def prompt_limits(sc, j, start):
    lane = lax.broadcasted_iota(jnp.int32, start.shape, 1)
    first = jnp.sum(jnp.where(lane == 0, start, 0))
    return first // BLOCK, (prompt_block(sc, j) * ROWS + ROWS - 1) // BLOCK + 1


def reply_places(sc):
    column = lax.broadcasted_iota(jnp.int32, (1, 4 * STRIPE), 1)
    stripe = sum((column >= j * STRIPE).astype(jnp.int32) for j in range(1, 4))
    return reply_block(sc, stripe) * ROWS + jnp.bitwise_and(column, ROWS - 1)


def reply_seen(sc, key_at, place):
    key = key_at + lax.broadcasted_iota(jnp.int32, (BLOCK, place.shape[1]), 0)
    return (key < sc[4]) & (key <= place)


def prompt_places(sc, j):
    lane = lax.broadcasted_iota(jnp.int32, (1, STRIPE), 1)
    return prompt_block(sc, j) * ROWS + jnp.bitwise_and(lane, ROWS - 1)


def online(state, q, k, v, seen):
    top, total, acc = state
    scores = dot(k, q, NT) * LOG2
    if seen is not None:
        scores = jnp.where(seen, scores, MASKED)
    raised = jnp.maximum(top, jnp.max(scores, axis=0, keepdims=True))
    shrink = jnp.exp2(top - raised)
    p = jnp.exp2(scores - raised)
    total = total * shrink + jnp.sum(p, axis=0, keepdims=True)
    return raised, total, acc * shrink + dot(v, p.astype(bf16), TN)


def empty(n):
    return jnp.full((1, n), LOW, f32), jnp.zeros((1, n), f32), jnp.zeros((HD, n), f32)


def grads(q, g, lse, rd, k, v, seen):
    w = jnp.exp2(dot(k, q, NT) * LOG2 - lse)
    if seen is not None:
        w = jnp.where(seen, w, 0.0)
    ds = (w * (dot(v, g, NT) - rd)).astype(bf16)
    return dot(ds, q, NN), dot(w.astype(bf16), g, NN), dot(ds, k, TN)


def attend_body(sc, *refs):
    q_in, kv_in, tables = refs[0:4], refs[4:12], refs[12:16]
    back, keep, send = refs[16:20], refs[20], refs[21]
    (pq, pg, rq, rg, pk, pv, rk, rv, r_stat, p_stat, pdq, rdq, pdk, pdv, rdk, rdv,
     stat_m, stat_l, acc_r, p_out, r_out, note, bias) = refs[22:]
    z, x, core, b, length = sc[0], sc[1], sc[2], sc[3], sc[4]

    for s in range(4):
        at = pl.ds(pl.multiple_of(lax.rem(z + 4 - s, 4) * STRIPE, STRIPE), STRIPE)
        for i, ref in enumerate((pq, pg, rq, rg)):
            ref[at, :] = q_in[s][i * STRIPE : (i + 1) * STRIPE, :]
    counts = jnp.zeros((16, HD), f32)
    for s in range(4):
        xx = x_of(sc, s)
        for other in range(2):
            piece = kv_in[s * 2 + other]
            cc = core if other == 0 else 1 - core
            for t in range(4):
                zz = lax.rem(z + 4 - t, 4)
                to = part((zz * 8 + xx * 2 + cc) * ROWS)
                o = t * OWN + PKV
                rk[to, :] = piece[o : o + 64, :]
                rv[to, :] = piece[o + 64 : o + 128, :]
                for far in range(2):
                    bb = b if far == 0 else 1 - b
                    to = part(granule(s, zz, cc * 2 + bb))
                    o = t * OWN if far == 0 else 4 * OWN + t * PKV
                    pk[to, :] = piece[o : o + 64, :]
                    pv[to, :] = piece[o + 64 : o + 128, :]
                    told = piece[o + 128 : o + 144, :].astype(f32)
                    counts = counts + told
                    if s == 0 and other == 0 and far == 0:
                        note[pl.ds(zz, 1)] = told[None]

    lane = lax.broadcasted_iota(jnp.int32, (1, HD), 1)
    starts = [
        jnp.sum(jnp.where(lane == s, counts[0:1, :], 0.0)).astype(jnp.int32) for s in range(HEADS)
    ]

    reply_place = reply_places(sc)
    q_all = rq[...]

    def forward_reply(i, state):
        at = pl.ds(pl.multiple_of(i * BLOCK, BLOCK), BLOCK)
        return online(state, q_all, pk[at, :], pv[at, :], None)

    top, total, acc = lax.fori_loop(0, PROMPT // BLOCK, forward_reply, empty(4 * STRIPE))
    half = 2 * STRIPE
    for i in range(4):
        at = slice(i * BLOCK, (i + 1) * BLOCK)
        if i < 2:
            seen = reply_seen(sc, i * BLOCK, reply_place)
            top, total, acc = online((top, total, acc), q_all, rk[at, :], rv[at, :], seen)
            if i == 1:
                stat_m[0:1, :] = top
                stat_l[0:1, :] = total
                acc_r[...] = acc
                state = (top[:, half:], total[:, half:], acc[:, half:])
        else:
            seen = reply_seen(sc, i * BLOCK, reply_place[:, half:])
            state = online(state, rq[half:, :], rk[at, :], rv[at, :], seen)
    stat_m[0:1, half:] = state[0]
    stat_l[0:1, half:] = state[1]
    acc_r[:, half:] = state[2]
    total = stat_l[0:1, :]
    out = jnp.where(reply_place < length, acc_r[...] / total, 0.0).astype(bf16).astype(f32)
    r_stat[0:1, :] = stat_m[0:1, :] + jnp.log2(total)
    r_stat[1:2, :] = jnp.sum(out * rg[...].astype(f32).T, axis=0, keepdims=True)
    acc_r[...] = out
    r_out[...] = acc_r[...].T

    limits, seen_from, places = [], [], []
    for j in range(4):
        ids = note[j, 1:2, :].astype(jnp.int32)
        start = jnp.zeros((1, HD), jnp.int32)
        for s in range(1, HEADS):
            start = jnp.where(ids == s, starts[s], start)
        limits.append(prompt_limits(sc, j, start))
        seen_from.append(jnp.concatenate([start, start, start[:, :64]], axis=1))
        places.append(prompt_places(sc, j))
    stripes = [slice(j * STRIPE, (j + 1) * STRIPE) for j in range(4)]
    for pair in ((0, 1), (2, 3)):

        def forward_prompt(i, states, pair=pair):
            out = []
            for j, state in zip(pair, states):
                low, high = limits[j]
                k, v, seen = prompt_block_of(
                    sc, low + i, high, pk, pv, seen_from[j], places[j]
                )
                out.append(online(state, pq[stripes[j], :], k, v, seen))
            return tuple(out)

        steps = jnp.maximum(*[limits[j][1] - limits[j][0] for j in pair])
        states = lax.fori_loop(0, steps, forward_prompt, (empty(STRIPE),) * 2)
        for j, (top, total, acc) in zip(pair, states):
            out = (acc / total).astype(bf16).astype(f32)
            p_stat[j, 0:1, :] = top + jnp.log2(total)
            p_stat[j, 1:2, :] = jnp.sum(
                out * pg[stripes[j], :].astype(f32).T, axis=0, keepdims=True
            )
            p_out[stripes[j], :] = out.T
    for s in range(4):
        at = pl.ds(pl.multiple_of(lax.rem(z + 4 - s, 4) * STRIPE, STRIPE), STRIPE)
        back[s][0:STRIPE, :] = p_out[at, :].astype(bf16)
        back[s][STRIPE : 2 * STRIPE, :] = r_out[at, :].astype(bf16)

    pdq[...] = jnp.zeros_like(pdq)
    rdq[...] = jnp.zeros_like(rdq)
    bias[...] = jnp.zeros_like(bias)

    def backward_reply(i, carry):
        at = pl.ds(pl.multiple_of(i * BLOCK, BLOCK), BLOCK)
        dk, dv, dq = grads(
            rq[...], rg[...], r_stat[0:1, :], r_stat[1:2, :], pk[at, :], pv[at, :], None
        )
        pdk[at, :] = dk
        pdv[at, :] = dv
        rdq[...] += dq
        return carry

    lax.fori_loop(0, PROMPT // BLOCK, backward_reply, 0)
    for pair in ((0, 1), (2, 3)):

        def backward_prompt(i, carry, pair=pair):
            done = []
            for j in pair:
                low, high = limits[j]
                k, v, seen = prompt_block_of(sc, low + i, high, pk, pv, seen_from[j], places[j])
                done.append(
                    grads(pq[stripes[j], :], pg[stripes[j], :], p_stat[j, 0:1, :],
                          p_stat[j, 1:2, :], k, v, seen)
                )
            for j, (dk, dv, dq) in zip(pair, done):
                at = jnp.minimum(limits[j][0] + i, PROMPT // BLOCK - 1)
                for n, rows in enumerate(prompt_rows(sc, at)):
                    pdk[rows, :] += dk[n * 256 : (n + 1) * 256, :]
                    pdv[rows, :] += dv[n * 256 : (n + 1) * 256, :]
                pdq[stripes[j], :] += dq
            return carry

        steps = jnp.maximum(*[limits[j][1] - limits[j][0] for j in pair])
        lax.fori_loop(0, steps, backward_prompt, 0)
    for i in range(4):
        at = slice(i * BLOCK, (i + 1) * BLOCK)
        cols = slice(0 if i < 2 else half, 4 * STRIPE)
        dk, dv, dq = grads(
            rq[cols, :], rg[cols, :], r_stat[0:1, cols], r_stat[1:2, cols], rk[at, :], rv[at, :],
            reply_seen(sc, i * BLOCK, reply_place[:, cols]),
        )
        rdk[at, :] = dk
        rdv[at, :] = dv
        rdq[cols, :] += dq

    coarse_cos, coarse_sin, fine_cos, fine_sin = tables

    def add(keys, values, row, block, sums):
        key = keys[pl.ds(pl.multiple_of(row, 256), 256), :]
        value = values[pl.ds(pl.multiple_of(row, 256), 256), :]
        for i in range(4):
            cut = slice(i * ROWS, (i + 1) * ROWS)
            at = pl.ds(block + i, 1)
            sums = (
                sums[0] + key[cut] * coarse_cos[at, :],
                sums[1] + key[cut] * coarse_sin[at, :],
                sums[2] + value[cut],
            )
        return sums

    sums = (jnp.zeros((ROWS, HD), f32),) * 3
    for s in range(4):
        sums = lax.fori_loop(
            0, 4, lambda zz, c, s=s: add(pdk, pdv, granule(s, zz), zz * 16 + x_of(sc, s) * 4, c), sums
        )
    sums = lax.fori_loop(0, 8, lambda i, c: add(rdk, rdv, i * 256, PROMPT // ROWS + i * 4, c), sums)
    key_sum = unrotate(sums[0] + pltpu.roll(sums[1], HD // 2, 1), fine_cos[...], fine_sin[...])
    bias[5:6, :] = jnp.sum(key_sum, axis=0, keepdims=True) * SCALE
    bias[6:7, :] = jnp.sum(sums[2], axis=0, keepdims=True)
    for s in range(4):
        zz = lax.rem(z + 4 - s, 4)
        for i, (ref, block) in enumerate(
            ((pdq, prompt_block(sc, zz)), (rdq, PROMPT // ROWS + reply_block(sc, zz)))
        ):
            cosine, sine = turn(tables, block)
            for m in range(GROUP):
                at = part(zz * STRIPE + m * ROWS)
                pre = unrotate(ref[at, :] * SCALE, cosine, sine)
                bias[m : m + 1, :] += jnp.sum(pre, axis=0, keepdims=True)
                o = (2 + i) * STRIPE + m * ROWS
                back[s][o : o + ROWS, :] = pre.astype(bf16)

    for s in range(4):
        xx = lax.rem(x + s, 4)
        for t in range(4):
            zz = lax.rem(z + t, 4)
            for far in range(2):
                bb = b if far == 0 else 1 - b
                own = part(granule((4 - s) % 4, zz, core * 2 + bb))
                theirs = part(granule((4 - s) % 4, zz, (1 - core) * 2 + bb))
                o = s * TERMS + far * 512 + t * ROWS
                keep[o : o + 64, :] = (pdk[own, :] * SCALE).astype(bf16)
                keep[o + 256 : o + 320, :] = pdv[own, :].astype(bf16)
                send[o : o + 64, :] = (pdk[theirs, :] * SCALE).astype(bf16)
                send[o + 256 : o + 320, :] = pdv[theirs, :].astype(bf16)
            own = part((zz * 8 + xx * 2 + core) * ROWS)
            theirs = part((zz * 8 + xx * 2 + 1 - core) * ROWS)
            o = s * TERMS + 1024 + t * ROWS
            keep[o : o + 64, :] = (rdk[own, :] * SCALE).astype(bf16)
            keep[o + 256 : o + 320, :] = rdv[own, :].astype(bf16)
            send[o : o + 64, :] = (rdk[theirs, :] * SCALE).astype(bf16)
            send[o + 256 : o + 320, :] = rdv[theirs, :].astype(bf16)
    words = two_words(bias[...])
    keep[4 * TERMS :, :] = words
    send[4 * TERMS :, :] = words


def two_words(x):
    high = x.astype(bf16).astype(f32)
    return jnp.concatenate([high, x - high], axis=0).astype(bf16)


def one_word(x):
    x = x.astype(f32)
    return x[0:8] + x[8:16]


def along_core_body(keep, got, near, p1, p2, p3, bias):
    at = slice(4 * TERMS, 4 * TERMS + 16)
    bias[...] = one_word(keep[at, :]) + one_word(got[at, :])
    for i, out in enumerate((near, p1, p2, p3)):
        at = slice(i * TERMS, (i + 1) * TERMS)
        out[...] = (keep[at, :].astype(f32) + got[at, :].astype(f32)).astype(out.dtype)


def along_x_body(after, own, r1, r2, r3, b0, b1, b2, b3, p_own, r_own, p_far, bias):
    total = own[...] + (r1[...].astype(f32) + r2[...].astype(f32) + r3[...].astype(f32))
    words = two_words((b0[...] + b2[...]) + (b1[...] + b3[...]))
    p_own[...] = total[0:512]
    r_own[...] = total[1024:1536]
    p_far[0:512, :] = total[512:1024].astype(bf16)
    p_far[512:528, :] = words
    bias[...] = one_word(words)


def settle_body(sc, p_own, r_own, p_far, b0, t0, t1, t2, t3, *outs):
    tables = (t0, t1, t2, t3)
    z = sc[0]
    words = two_words(b0[...] + one_word(p_far[512:528, :]))
    for t, out in enumerate(outs):
        zz = lax.rem(z + t, 4)
        o = t * ROWS
        key = p_own[o : o + 64, :] + p_far[o : o + 64, :].astype(f32)
        out[0:64, :] = unrotate(key, *turn(tables, prompt_block(sc, zz))).astype(bf16)
        value = p_own[o + 256 : o + 320, :] + p_far[o + 256 : o + 320, :].astype(f32)
        out[64:128, :] = value.astype(bf16)
        block = PROMPT // ROWS + reply_block(sc, zz)
        out[128:192, :] = unrotate(r_own[o : o + 64, :], *turn(tables, block)).astype(bf16)
        out[192:256, :] = r_own[o + 256 : o + 320, :].astype(bf16)
        out[256:272, :] = words


def finish_body(sc, *refs):
    pieces, outs, (qsum, ksum, vsum) = refs[0:4], refs[4:8], refs[8:]
    z = sc[0]
    for t, piece in enumerate(pieces):
        h = lax.rem(z + 4 - t, 4)
        for i, out in enumerate(outs):
            out[:, lanes(h)] = piece[i * ROWS : (i + 1) * ROWS, :]
        bias = one_word(piece[256:272, :])
        for m in range(GROUP):
            qsum[:, lanes(h * GROUP + m)] = bias[m : m + 1]
        ksum[:, lanes(h)] = bias[5:6]
        vsum[:, lanes(h)] = bias[6:7]


def gather_heads_body(step, sc, *refs):
    pieces, outs = refs[:4], refs[4:]
    z = sc[0]
    for s, piece in enumerate(pieces):
        h = lax.rem(z + (s * step) % 4, 4)
        width = piece.shape[0] // ROWS // len(outs)
        for i, out in enumerate(outs):
            for m in range(width):
                o = (i * width + m) * ROWS
                out[:, lanes(h * width + m)] = piece[o : o + ROWS, :]


def call(body, n_in, outs, scratch=(), scalars=True, anywhere=(), us=1, mib=16):
    spec = pl.BlockSpec(memory_space=pltpu.VMEM)
    first = [pl.BlockSpec(memory_space=pltpu.SMEM)] if scalars else []
    ins = [pl.BlockSpec(memory_space=pl.ANY) if i in anywhere else spec for i in range(n_in)]
    return pl.pallas_call(
        body,
        in_specs=first + ins,
        out_specs=[spec] * len(outs),
        out_shape=[jax.ShapeDtypeStruct(s, t) for s, t in outs],
        scratch_shapes=list(scratch),
        cost_estimate=pl.CostEstimate(
            flops=us * 1000000, bytes_accessed=us * 3000000, transcendentals=0
        ),
        compiler_params=pltpu.CompilerParams(vmem_limit_bytes=mib * 1024 * 1024),
    )


def shift(v, axis, s):
    n = lax.axis_size(axis)
    return lax.ppermute(v, axis, [(i, (i + s) % n) for i in range(n)])


def on_device(pq, pk, pv, pg, rq, rk, rv, rg, qbias, kbias, vbias, segments, lengths):
    sc = jnp.stack(
        [lax.axis_index(a) for a in ("z", "x", "core", "branch")] + [lengths[0, 0]]
    ).astype(jnp.int32)
    tables = angle_tables()
    bias = jnp.concatenate([qbias, kbias, vbias])[None]
    kv = call(prepare_kv_body, 10, [((OWN, HD), bf16)] * 4, mib=56)(
        sc, pk[0], pv[0], rk[0, 0], rv[0, 0], bias, segments, *tables
    )
    q = call(prepare_q_body, 9, [((4 * STRIPE, HD), bf16)] * 4, mib=56)(
        sc, pq[0], pg[0], rq[0, 0], rg[0, 0], bias, *tables
    )
    kv = jnp.stack([kv[0]] + [shift(kv[s], "z", s) for s in (1, 2, 3)])
    kv, q = lax.optimization_barrier((kv, q))
    q = [q[0]] + [shift(q[s], "z", s) for s in (1, 2, 3)]
    far = shift(kv[:, :PKV].reshape(4 * PKV, HD), "branch", 1)
    kv = jnp.concatenate([kv.reshape(4 * OWN, HD), far])
    across = [kv] + [shift(kv, "x", s) for s in (1, 2, 3)]
    across[2], q = lax.optimization_barrier((across[2], q))
    pieces = [v for piece in across for v in (piece, shift(piece, "core", 1))]

    rows = 4 * STRIPE
    outs = call(
        attend_body,
        16,
        [((rows, HD), bf16)] * 4 + [((4 * TERMS + 16, HD), bf16)] * 2,
        [pltpu.VMEM((rows, HD), bf16)] * 4
        + [pltpu.VMEM((PROMPT, HD), bf16)] * 2
        + [pltpu.VMEM((REPLY, HD), bf16)] * 2
        + [pltpu.VMEM((8, rows), f32), pltpu.VMEM((4, 8, STRIPE), f32)]
        + [pltpu.VMEM((rows, HD), f32)] * 2
        + [pltpu.VMEM((PROMPT, HD), f32)] * 2
        + [pltpu.VMEM((REPLY, HD), f32)] * 2
        + [pltpu.VMEM((8, rows), f32)] * 2
        + [pltpu.VMEM((HD, rows), f32)]
        + [pltpu.VMEM((rows, HD), f32)] * 2
        + [pltpu.VMEM((4, 16, HD), f32), pltpu.VMEM((8, HD), f32)],
        us=60,
        mib=40,
    )(sc, *q, *pieces, *tables)
    back, (keep, send) = outs[:4], outs[4:]
    own, *parts, bias = call(
        along_core_body,
        2,
        [((TERMS, HD), f32)] + [((TERMS, HD), bf16)] * 3 + [((8, HD), f32)],
        scalars=False,
        us=2,
    )(keep, shift(send, "core", 1))
    back = [back[0]] + [shift(back[s], "z", -s) for s in (1, 2, 3)]
    parts = [shift(parts[s - 1], "x", s) for s in (1, 2, 3)]
    bias = bias + shift(bias, "dp", 1)
    biases = [bias] + [shift(bias, "x", s) for s in (1, 2, 3)]
    wide = ((ROWS, HEADS * GROUP * HD), bf16)
    p_out, r_out, p_dq, r_dq = call(functools.partial(gather_heads_body, 1), 4, [wide] * 4, us=2)(
        sc, *back
    )
    p_own, r_own, p_far, bias = call(
        along_x_body,
        9,
        [((512, HD), f32)] * 2 + [((528, HD), bf16), ((8, HD), f32)],
        scalars=False,
        anywhere=(0,),
        us=2,
    )(p_out, own, *parts, *biases)
    p_far = shift(p_far, "branch", 1)
    dkv = call(settle_body, 8, [((4 * ROWS + 16, HD), bf16)] * 4)(
        sc, p_own, r_own, p_far, bias, *tables
    )
    dkv = [dkv[0]] + [shift(dkv[t], "z", t) for t in (1, 2, 3)]
    narrow = ((ROWS, HEADS * HD), bf16)
    p_dk, p_dv, r_dk, r_dv, qsum, ksum, vsum = call(
        finish_body,
        4,
        [narrow] * 4 + [((1, HEADS * GROUP * HD), f32)] + [((1, HEADS * HD), f32)] * 2,
    )(sc, *dkv)
    return (
        p_out[None],
        r_out[None, None],
        p_dq[None],
        p_dk[None],
        p_dv[None],
        r_dq[None, None],
        r_dk[None, None],
        r_dv[None, None],
        qsum.reshape(-1),
        ksum.reshape(-1),
        vsum.reshape(-1),
    )


def solution(mesh):
    fine = Mesh(mesh.devices.reshape(2, 4, 4, 2, 2), ("dp", "z", "x", "core", "branch"))
    prompt = P("dp", ("z", "x", "core", "branch"), None)
    reply = P("dp", "branch", ("z", "x", "core"), None)
    return jax.shard_map(
        on_device,
        mesh=fine,
        in_specs=(prompt,) * 4
        + (reply,) * 4
        + (P(),) * 3
        + (P("dp", ("z", "x", "core", "branch")), P("dp", "branch")),
        out_specs=(prompt, reply, prompt, prompt, prompt, reply, reply, reply, P(), P(), P()),
        check_vma=False,
    )
```

```python
import functools

import jax
import jax.numpy as jnp
import numpy as np
from jax import lax
from jax.experimental import pallas as pl
from jax.experimental.pallas import tpu as pltpu
from jax.sharding import Mesh
from jax.sharding import PartitionSpec as P

HEADS = 4
GROUP = 5
HD = 128
ROWS = 64
STRIPE = GROUP * ROWS
PROMPT = 4096
REPLY = 2048
BLOCK = 512
SCALE = HD**-0.5
LOG2 = float(SCALE * np.log2(np.e))
LOW = -1e30
MASKED = -3e38
KV = 2 * ROWS
PKV = KV + 16
OWN = PKV + KV
PIECE = 4 * OWN + 4 * PKV
TERMS = 1536

bf16 = jnp.bfloat16
f32 = jnp.float32
NT = (((1,), (1,)), ((), ()))
NN = (((1,), (0,)), ((), ()))
TN = (((0,), (0,)), ((), ()))


def dot(a, b, dims):
    return lax.dot_general(a, b, dims, preferred_element_type=f32)


def angle_tables():
    frequency = 1000000.0 ** (-(np.arange(HD // 2) * 2.0 / HD))
    frequency = np.concatenate([frequency, frequency])
    sign = np.where(np.arange(HD) < HD // 2, -1.0, 1.0)
    coarse = np.arange((PROMPT + REPLY) // ROWS)[:, None] * ROWS * frequency
    fine = np.arange(ROWS)[:, None] * frequency
    return [
        jnp.asarray(t.astype(np.float32))
        for t in (np.cos(coarse), np.sin(coarse) * sign, np.cos(fine), np.sin(fine) * sign)
    ]


def turn(tables, block):
    coarse_cos, coarse_sin, fine_cos, fine_sin = tables
    ca, sa = coarse_cos[pl.ds(block, 1), :], coarse_sin[pl.ds(block, 1), :]
    cb, sb = fine_cos[...], fine_sin[...]
    return ca * cb - sa * sb, sa * cb + ca * sb


def rotate(x, cosine, sine):
    return x * cosine + pltpu.roll(x, HD // 2, 1) * sine


def unrotate(x, cosine, sine):
    return x * cosine - pltpu.roll(x, HD // 2, 1) * sine


def prompt_block(sc, z):
    return z * 16 + sc[1] * 4 + sc[2] * 2 + sc[3]


def reply_block(sc, z):
    return z * 8 + sc[1] * 2 + sc[2]


def part(i):
    return pl.ds(pl.multiple_of(i, ROWS), ROWS)


def lanes(i):
    return pl.ds(pl.multiple_of(i * HD, HD), HD)


def prepare_kv_body(sc, pk, pv, rk, rv, bias, seg, t0, t1, t2, t3, *outs):
    tables = (t0, t1, t2, t3)
    z = sc[0]
    prompt_turn = turn(tables, prompt_block(sc, z))
    reply_turn = turn(tables, PROMPT // ROWS + reply_block(sc, z))
    ids = jnp.concatenate([seg[...], seg[...]], axis=1)
    row = lax.broadcasted_iota(jnp.int32, (16, HD), 0)
    lane = lax.broadcasted_iota(jnp.int32, (16, HD), 1)
    note = jnp.zeros((16, HD), f32)
    for s in range(1, HEADS):
        below = jnp.sum((ids < s).astype(f32), axis=1, keepdims=True) * 0.5
        note = jnp.where((row == 0) & (lane == s), below, note)
    note = jnp.where(row == 1, ids.astype(f32), note).astype(bf16)
    for s, out in enumerate(outs):
        h = lax.rem(z + s, HEADS)
        at = lanes(h)
        kb, vb = bias[pl.ds(20 + h, 1), :], bias[pl.ds(24 + h, 1), :]
        out[0:64, :] = rotate(pk[:, at].astype(f32) + kb, *prompt_turn).astype(bf16)
        out[64:128, :] = (pv[:, at].astype(f32) + vb).astype(bf16)
        out[128:144, :] = note
        out[144:208, :] = rotate(rk[:, at].astype(f32) + kb, *reply_turn).astype(bf16)
        out[208:272, :] = (rv[:, at].astype(f32) + vb).astype(bf16)


def prepare_q_body(sc, pq, pg, rq, rg, bias, t0, t1, t2, t3, *outs):
    tables = (t0, t1, t2, t3)
    z = sc[0]
    prompt_turn = turn(tables, prompt_block(sc, z))
    reply_turn = turn(tables, PROMPT // ROWS + reply_block(sc, z))
    place = reply_block(sc, z) * ROWS + lax.broadcasted_iota(jnp.int32, (ROWS, HD), 0)
    valid = place < sc[4]
    for s, out in enumerate(outs):
        h = lax.rem(z + s, HEADS) * GROUP
        for m in range(GROUP):
            at = lanes(h + m)
            qb = bias[pl.ds(h + m, 1), :]
            o = m * ROWS
            out[o : o + 64, :] = rotate(pq[:, at].astype(f32) + qb, *prompt_turn).astype(bf16)
            o += STRIPE
            out[o : o + 64, :] = pg[:, at]
            o += STRIPE
            out[o : o + 64, :] = rotate(rq[:, at].astype(f32) + qb, *reply_turn).astype(bf16)
            o += STRIPE
            out[o : o + 64, :] = jnp.where(valid, rg[:, at].astype(f32), 0.0).astype(bf16)


def granule(s, zz, sub=0):
    return s * 1024 + zz * 256 + sub * ROWS


def x_of(sc, s):
    return lax.rem(sc[1] + 4 - s, 4)


def prompt_rows(sc, i):
    pair = [granule(lax.rem(sc[1] + 4 - lax.rem(i, 2) * 2 - n, 4), i // 2) for n in range(2)]
    return [pl.ds(pl.multiple_of(row, 256), 256) for row in pair]


def prompt_block_of(sc, i, there, pk, pv, start, place):
    rows = prompt_rows(sc, i)
    key = lax.broadcasted_iota(jnp.int32, (BLOCK, STRIPE), 0)
    start, place = start - i * BLOCK, jnp.where(there, place - i * BLOCK, -1)
    k, v = [jnp.concatenate([ref[at, :] for at in rows], axis=0) for ref in (pk, pv)]
    return k, v, (key >= start) & (key <= place)


def prompt_limits(sc, j, start):
    lane = lax.broadcasted_iota(jnp.int32, start.shape, 1)
    first = jnp.sum(jnp.where(lane == 0, start, 0))
    return first // BLOCK, (prompt_block(sc, j) * ROWS + ROWS - 1) // BLOCK + 1


def reply_places(sc):
    column = lax.broadcasted_iota(jnp.int32, (1, 4 * STRIPE), 1)
    stripe = sum((column >= j * STRIPE).astype(jnp.int32) for j in range(1, 4))
    return reply_block(sc, stripe) * ROWS + jnp.bitwise_and(column, ROWS - 1)


def reply_seen(sc, key_at, place):
    key = lax.broadcasted_iota(jnp.int32, (BLOCK, place.shape[1]), 0)
    return key <= jnp.minimum(place, sc[4] - 1) - key_at


def prompt_places(sc, j):
    lane = lax.broadcasted_iota(jnp.int32, (1, STRIPE), 1)
    return prompt_block(sc, j) * ROWS + jnp.bitwise_and(lane, ROWS - 1)


def online(state, q, k, v, seen):
    top, total, acc = state
    scores = dot(k, q, NT) * LOG2
    if seen is not None:
        scores = jnp.where(seen, scores, MASKED)
    raised = jnp.maximum(top, jnp.max(scores, axis=0, keepdims=True))
    shrink = jnp.exp2(top - raised)
    p = jnp.exp2(scores - raised)
    total = total * shrink + jnp.sum(p, axis=0, keepdims=True)
    return raised, total, acc * shrink + dot(v, p.astype(bf16), TN)


def empty(n):
    return jnp.full((1, n), LOW, f32), jnp.zeros((1, n), f32), jnp.zeros((HD, n), f32)


def grads(q, g, lse, rd, k, v, seen):
    w = jnp.exp2(dot(k, q, NT) * LOG2 - lse)
    if seen is not None:
        w = jnp.where(seen, w, 0.0)
    ds = (w * (dot(v, g, NT) - rd)).astype(bf16)
    return dot(ds, q, NN), dot(w.astype(bf16), g, NN), dot(ds, k, TN)


def attend_body(sc, *refs):
    q_in, kv_in, tables = refs[0:4], refs[4:12], refs[12:16]
    back, keep, send = refs[16:20], refs[20], refs[21]
    (pq, pg, rq, rg, pk, pv, rk, rv, r_stat, p_stat, pdq, rdq, pdk, pdv, rdk, rdv,
     stat_m, stat_l, acc_r, p_out, r_out, note, bias, seen_from) = refs[22:46]
    p_top, p_total, p_acc = refs[46:48], refs[48:50], refs[50:52]
    z, x, core, b, length = sc[0], sc[1], sc[2], sc[3], sc[4]

    for s in range(4):
        at = pl.ds(pl.multiple_of(lax.rem(z + 4 - s, 4) * STRIPE, STRIPE), STRIPE)
        for i, ref in enumerate((pq, pg, rq, rg)):
            ref[at, :] = q_in[s][i * STRIPE : (i + 1) * STRIPE, :]
    counts = jnp.zeros((16, HD), f32)
    for s in range(4):
        xx = x_of(sc, s)
        for other in range(2):
            piece = kv_in[s * 2 + other]
            cc = core if other == 0 else 1 - core
            for t in range(4):
                zz = lax.rem(z + 4 - t, 4)
                to = part((zz * 8 + xx * 2 + cc) * ROWS)
                o = t * OWN + PKV
                rk[to, :] = piece[o : o + 64, :]
                rv[to, :] = piece[o + 64 : o + 128, :]
                for far in range(2):
                    bb = b if far == 0 else 1 - b
                    to = part(granule(s, zz, cc * 2 + bb))
                    o = t * OWN if far == 0 else 4 * OWN + t * PKV
                    pk[to, :] = piece[o : o + 64, :]
                    pv[to, :] = piece[o + 64 : o + 128, :]
                    told = piece[o + 128 : o + 144, :].astype(f32)
                    counts = counts + told
                    if s == 0 and other == 0 and far == 0:
                        note[pl.ds(zz, 1)] = told[None]

    lane = lax.broadcasted_iota(jnp.int32, (1, HD), 1)
    starts = [
        jnp.sum(jnp.where(lane == s, counts[0:1, :], 0.0)).astype(jnp.int32) for s in range(HEADS)
    ]

    reply_place = reply_places(sc)
    q_all = rq[...]

    def forward_reply(i, state):
        at = pl.ds(pl.multiple_of(i * 2 * BLOCK, 2 * BLOCK), 2 * BLOCK)
        return online(state, q_all, pk[at, :], pv[at, :], None)

    top, total, acc = lax.fori_loop(0, PROMPT // BLOCK // 2, forward_reply, empty(4 * STRIPE), unroll=2)
    half = 2 * STRIPE
    for i in range(4):
        at = slice(i * BLOCK, (i + 1) * BLOCK)
        if i < 2:
            seen = reply_seen(sc, i * BLOCK, reply_place)
            top, total, acc = online((top, total, acc), q_all, rk[at, :], rv[at, :], seen)
            if i == 1:
                stat_m[0:1, :] = top
                stat_l[0:1, :] = total
                acc_r[...] = acc
                state = (top[:, half:], total[:, half:], acc[:, half:])
        else:
            seen = reply_seen(sc, i * BLOCK, reply_place[:, half:])
            state = online(state, rq[half:, :], rk[at, :], rv[at, :], seen)
    stat_m[0:1, half:] = state[0]
    stat_l[0:1, half:] = state[1]
    acc_r[:, half:] = state[2]
    total = stat_l[0:1, :]
    out = jnp.where(reply_place < length, acc_r[...] / total, 0.0).astype(bf16).astype(f32)
    r_stat[0:1, :] = stat_m[0:1, :] + jnp.log2(total)
    r_stat[1:2, :] = jnp.sum(out * rg[...].astype(f32).T, axis=0, keepdims=True)
    acc_r[...] = out
    r_out[...] = acc_r[...].T

    lows, ends, total_blocks = [], [], 0
    for j in range(4):
        ids = note[j, 1:2, :].astype(jnp.int32)
        start = jnp.zeros((1, HD), jnp.int32)
        for s in range(1, HEADS):
            start = jnp.where(ids == s, starts[s], start)
        low, high = prompt_limits(sc, j, start)
        lows.append(low)
        total_blocks = total_blocks + high - low
        ends.append(total_blocks)
        seen_from[j, 0:1, :] = jnp.concatenate([start, start, start[:, :64]], axis=1)
    half_list = (total_blocks + 1) // 2

    def listed(i, side):
        n = i + side * half_list
        j, low, before = 0, lows[0], 0
        for k in range(3):
            later = n >= ends[k]
            j = jnp.where(later, k + 1, j)
            low = jnp.where(later, lows[k + 1], low)
            before = jnp.where(later, ends[k], before)
        there = n < total_blocks
        return j, jnp.where(there, low + n - before, 0), there

    def stripe_rows(j):
        return pl.ds(pl.multiple_of(j * STRIPE, STRIPE), STRIPE)

    def seen_block(j, block, there):
        return prompt_block_of(
            sc, block, there, pk, pv, seen_from[j, 0:1, :], prompt_places(sc, j)
        )

    for side in range(2):
        p_top[side][...] = jnp.full_like(p_top[side], LOW)
        p_total[side][...] = jnp.zeros_like(p_total[side])
        p_acc[side][...] = jnp.zeros_like(p_acc[side])

    def forward_prompt(i, carry):
        for side in range(2):
            j, block, there = listed(i, side)
            k, v, seen = seen_block(j, block, there)
            state = p_top[side][j, 0:1, :], p_total[side][j, 0:1, :], p_acc[side][j]
            top, total, acc = online(state, pq[stripe_rows(j), :], k, v, seen)
            p_top[side][j, 0:1, :] = top
            p_total[side][j, 0:1, :] = total
            p_acc[side][j] = acc
        return carry

    lax.fori_loop(0, half_list, forward_prompt, 0)
    for j in range(4):
        rows = slice(j * STRIPE, (j + 1) * STRIPE)
        tops = [p_top[side][j, 0:1, :] for side in range(2)]
        top = jnp.maximum(*tops)
        shrinks = [jnp.exp2(t - top) for t in tops]
        total = sum(p_total[side][j, 0:1, :] * shrinks[side] for side in range(2))
        acc = sum(p_acc[side][j] * shrinks[side] for side in range(2))
        out = (acc / total).astype(bf16).astype(f32)
        p_stat[j, 0:1, :] = top + jnp.log2(total)
        p_stat[j, 1:2, :] = jnp.sum(out * pg[rows, :].astype(f32).T, axis=0, keepdims=True)
        p_out[rows, :] = out.T
    for s in range(4):
        at = pl.ds(pl.multiple_of(lax.rem(z + 4 - s, 4) * STRIPE, STRIPE), STRIPE)
        back[s][0:STRIPE, :] = p_out[at, :].astype(bf16)
        back[s][STRIPE : 2 * STRIPE, :] = r_out[at, :].astype(bf16)

    pdq[...] = jnp.zeros_like(pdq)
    rdq[...] = jnp.zeros_like(rdq)
    bias[...] = jnp.zeros_like(bias)

    def backward_reply(i, carry):
        at = pl.ds(pl.multiple_of(i * BLOCK, BLOCK), BLOCK)
        dk, dv, dq = grads(
            rq[...], rg[...], r_stat[0:1, :], r_stat[1:2, :], pk[at, :], pv[at, :], None
        )
        pdk[at, :] = dk
        pdv[at, :] = dv
        rdq[...] += dq
        return carry

    lax.fori_loop(0, PROMPT // BLOCK, backward_reply, 0, unroll=2)

    def backward_prompt(i, carry):
        done = []
        for side in range(2):
            j, block, there = listed(i, side)
            k, v, seen = seen_block(j, block, there)
            rows = stripe_rows(j)
            terms = grads(
                pq[rows, :], pg[rows, :], p_stat[j, 0:1, :], p_stat[j, 1:2, :], k, v, seen
            )
            done.append((rows, prompt_rows(sc, block), terms))
        for rows, keys, (dk, dv, dq) in done:
            for n, at in enumerate(keys):
                pdk[at, :] += dk[n * 256 : (n + 1) * 256, :]
                pdv[at, :] += dv[n * 256 : (n + 1) * 256, :]
            pdq[rows, :] += dq
        return carry

    lax.fori_loop(0, half_list, backward_prompt, 0)
    for i in range(4):
        at = slice(i * BLOCK, (i + 1) * BLOCK)
        cols = slice(0 if i < 2 else half, 4 * STRIPE)
        dk, dv, dq = grads(
            rq[cols, :], rg[cols, :], r_stat[0:1, cols], r_stat[1:2, cols], rk[at, :], rv[at, :],
            reply_seen(sc, i * BLOCK, reply_place[:, cols]),
        )
        rdk[at, :] = dk
        rdv[at, :] = dv
        rdq[cols, :] += dq

    coarse_cos, coarse_sin, fine_cos, fine_sin = tables

    def add(keys, values, row, block, sums):
        key = keys[pl.ds(pl.multiple_of(row, 256), 256), :]
        value = values[pl.ds(pl.multiple_of(row, 256), 256), :]
        for i in range(4):
            cut = slice(i * ROWS, (i + 1) * ROWS)
            at = pl.ds(block + i, 1)
            sums = (
                sums[0] + key[cut] * coarse_cos[at, :],
                sums[1] + key[cut] * coarse_sin[at, :],
                sums[2] + value[cut],
            )
        return sums

    sums = (jnp.zeros((ROWS, HD), f32),) * 3
    for s in range(4):
        sums = lax.fori_loop(
            0, 4, lambda zz, c, s=s: add(pdk, pdv, granule(s, zz), zz * 16 + x_of(sc, s) * 4, c), sums
        )
    sums = lax.fori_loop(0, 8, lambda i, c: add(rdk, rdv, i * 256, PROMPT // ROWS + i * 4, c), sums)
    key_sum = unrotate(sums[0] + pltpu.roll(sums[1], HD // 2, 1), fine_cos[...], fine_sin[...])
    bias[5:6, :] = jnp.sum(key_sum, axis=0, keepdims=True) * SCALE
    bias[6:7, :] = jnp.sum(sums[2], axis=0, keepdims=True)
    for s in range(4):
        zz = lax.rem(z + 4 - s, 4)
        for i, (ref, block) in enumerate(
            ((pdq, prompt_block(sc, zz)), (rdq, PROMPT // ROWS + reply_block(sc, zz)))
        ):
            cosine, sine = turn(tables, block)
            for m in range(GROUP):
                at = part(zz * STRIPE + m * ROWS)
                pre = unrotate(ref[at, :] * SCALE, cosine, sine)
                bias[m : m + 1, :] += jnp.sum(pre, axis=0, keepdims=True)
                o = (2 + i) * STRIPE + m * ROWS
                back[s][o : o + ROWS, :] = pre.astype(bf16)

    for s in range(4):
        xx = lax.rem(x + s, 4)
        for t in range(4):
            zz = lax.rem(z + t, 4)
            for far in range(2):
                bb = b if far == 0 else 1 - b
                own = part(granule((4 - s) % 4, zz, core * 2 + bb))
                theirs = part(granule((4 - s) % 4, zz, (1 - core) * 2 + bb))
                o = s * TERMS + far * 512 + t * ROWS
                keep[o : o + 64, :] = (pdk[own, :] * SCALE).astype(bf16)
                keep[o + 256 : o + 320, :] = pdv[own, :].astype(bf16)
                send[o : o + 64, :] = (pdk[theirs, :] * SCALE).astype(bf16)
                send[o + 256 : o + 320, :] = pdv[theirs, :].astype(bf16)
            own = part((zz * 8 + xx * 2 + core) * ROWS)
            theirs = part((zz * 8 + xx * 2 + 1 - core) * ROWS)
            o = s * TERMS + 1024 + t * ROWS
            keep[o : o + 64, :] = (rdk[own, :] * SCALE).astype(bf16)
            keep[o + 256 : o + 320, :] = rdv[own, :].astype(bf16)
            send[o : o + 64, :] = (rdk[theirs, :] * SCALE).astype(bf16)
            send[o + 256 : o + 320, :] = rdv[theirs, :].astype(bf16)
    words = two_words(bias[...])
    keep[4 * TERMS :, :] = words
    send[4 * TERMS :, :] = words


def two_words(x):
    high = x.astype(bf16).astype(f32)
    return jnp.concatenate([high, x - high], axis=0).astype(bf16)


def one_word(x):
    x = x.astype(f32)
    return x[0:8] + x[8:16]


def along_core_body(keep, got, near, p1, p2, p3, bias):
    at = slice(4 * TERMS, 4 * TERMS + 16)
    bias[...] = one_word(keep[at, :]) + one_word(got[at, :])
    for i, out in enumerate((near, p1, p2, p3)):
        at = slice(i * TERMS, (i + 1) * TERMS)
        out[...] = (keep[at, :].astype(f32) + got[at, :].astype(f32)).astype(out.dtype)


def along_x_body(after, own, r1, r2, r3, b0, b1, b2, b3, p_own, r_own, p_far, bias):
    total = own[...] + (r1[...].astype(f32) + r2[...].astype(f32) + r3[...].astype(f32))
    words = two_words((b0[...] + b2[...]) + (b1[...] + b3[...]))
    p_own[...] = total[0:512]
    r_own[...] = total[1024:1536]
    p_far[0:512, :] = total[512:1024].astype(bf16)
    p_far[512:528, :] = words
    bias[...] = one_word(words)


def settle_body(sc, p_own, r_own, p_far, b0, t0, t1, t2, t3, *outs):
    tables = (t0, t1, t2, t3)
    z = sc[0]
    words = two_words(b0[...] + one_word(p_far[512:528, :]))
    for t, out in enumerate(outs):
        zz = lax.rem(z + t, 4)
        o = t * ROWS
        key = p_own[o : o + 64, :] + p_far[o : o + 64, :].astype(f32)
        out[0:64, :] = unrotate(key, *turn(tables, prompt_block(sc, zz))).astype(bf16)
        value = p_own[o + 256 : o + 320, :] + p_far[o + 256 : o + 320, :].astype(f32)
        out[64:128, :] = value.astype(bf16)
        block = PROMPT // ROWS + reply_block(sc, zz)
        out[128:192, :] = unrotate(r_own[o : o + 64, :], *turn(tables, block)).astype(bf16)
        out[192:256, :] = r_own[o + 256 : o + 320, :].astype(bf16)
        out[256:272, :] = words


def finish_body(sc, *refs):
    pieces, outs, (qsum, ksum, vsum) = refs[0:4], refs[4:8], refs[8:]
    z = sc[0]
    for t, piece in enumerate(pieces):
        h = lax.rem(z + 4 - t, 4)
        for i, out in enumerate(outs):
            out[:, lanes(h)] = piece[i * ROWS : (i + 1) * ROWS, :]
        bias = one_word(piece[256:272, :])
        for m in range(GROUP):
            qsum[:, lanes(h * GROUP + m)] = bias[m : m + 1]
        ksum[:, lanes(h)] = bias[5:6]
        vsum[:, lanes(h)] = bias[6:7]


def gather_heads_body(step, sc, *refs):
    pieces, outs = refs[:4], refs[4:]
    z = sc[0]
    for s, piece in enumerate(pieces):
        h = lax.rem(z + (s * step) % 4, 4)
        width = piece.shape[0] // ROWS // len(outs)
        for i, out in enumerate(outs):
            for m in range(width):
                o = (i * width + m) * ROWS
                out[:, lanes(h * width + m)] = piece[o : o + ROWS, :]


def call(body, n_in, outs, scratch=(), scalars=True, anywhere=(), us=1, mib=16):
    spec = pl.BlockSpec(memory_space=pltpu.VMEM)
    first = [pl.BlockSpec(memory_space=pltpu.SMEM)] if scalars else []
    ins = [pl.BlockSpec(memory_space=pl.ANY) if i in anywhere else spec for i in range(n_in)]
    return pl.pallas_call(
        body,
        in_specs=first + ins,
        out_specs=[spec] * len(outs),
        out_shape=[jax.ShapeDtypeStruct(s, t) for s, t in outs],
        scratch_shapes=list(scratch),
        cost_estimate=pl.CostEstimate(
            flops=us * 1000000, bytes_accessed=us * 3000000, transcendentals=0
        ),
        compiler_params=pltpu.CompilerParams(vmem_limit_bytes=mib * 1024 * 1024),
    )


def shift(v, axis, s):
    n = lax.axis_size(axis)
    return lax.ppermute(v, axis, [(i, (i + s) % n) for i in range(n)])


def on_device(pq, pk, pv, pg, rq, rk, rv, rg, qbias, kbias, vbias, segments, lengths):
    sc = jnp.stack(
        [lax.axis_index(a) for a in ("z", "x", "core", "branch")] + [lengths[0, 0]]
    ).astype(jnp.int32)
    tables = angle_tables()
    bias = jnp.concatenate([qbias, kbias, vbias]).astype(f32).reshape(-1, HD)
    kv = call(prepare_kv_body, 10, [((OWN, HD), bf16)] * 4, mib=56)(
        sc, pk[0], pv[0], rk[0, 0], rv[0, 0], bias, segments, *tables
    )
    q = call(prepare_q_body, 9, [((4 * STRIPE, HD), bf16)] * 4, mib=56)(
        sc, pq[0], pg[0], rq[0, 0], rg[0, 0], bias, *tables
    )
    kv = jnp.stack([kv[0]] + [shift(kv[s], "z", s) for s in (1, 2, 3)])
    kv, q = lax.optimization_barrier((kv, q))
    q = [q[0]] + [shift(q[s], "z", s) for s in (1, 2, 3)]
    far = shift(kv[:, :PKV].reshape(4 * PKV, HD), "branch", 1)
    kv = jnp.concatenate([kv.reshape(4 * OWN, HD), far])
    across = [kv] + [shift(kv, "x", s) for s in (1, 2, 3)]
    across[2], q = lax.optimization_barrier((across[2], q))
    pieces = [v for piece in across for v in (piece, shift(piece, "core", 1))]

    rows = 4 * STRIPE
    outs = call(
        attend_body,
        16,
        [((rows, HD), bf16)] * 4 + [((4 * TERMS + 16, HD), bf16)] * 2,
        [pltpu.VMEM((rows, HD), bf16)] * 4
        + [pltpu.VMEM((PROMPT, HD), bf16)] * 2
        + [pltpu.VMEM((REPLY, HD), bf16)] * 2
        + [pltpu.VMEM((8, rows), f32), pltpu.VMEM((4, 8, STRIPE), f32)]
        + [pltpu.VMEM((rows, HD), f32)] * 2
        + [pltpu.VMEM((PROMPT, HD), f32)] * 2
        + [pltpu.VMEM((REPLY, HD), f32)] * 2
        + [pltpu.VMEM((8, rows), f32)] * 2
        + [pltpu.VMEM((HD, rows), f32)]
        + [pltpu.VMEM((rows, HD), f32)] * 2
        + [pltpu.VMEM((4, 16, HD), f32), pltpu.VMEM((8, HD), f32)]
        + [pltpu.VMEM((4, 8, STRIPE), jnp.int32)]
        + [pltpu.VMEM((4, 8, STRIPE), f32)] * 4
        + [pltpu.VMEM((4, HD, STRIPE), f32)] * 2,
        us=60,
        mib=40,
    )(sc, *q, *pieces, *tables)
    back, (keep, send) = outs[:4], outs[4:]
    own, *parts, bias = call(
        along_core_body,
        2,
        [((TERMS, HD), f32)] + [((TERMS, HD), bf16)] * 3 + [((8, HD), f32)],
        scalars=False,
        us=2,
    )(keep, shift(send, "core", 1))
    back = [back[0]] + [shift(back[s], "z", -s) for s in (1, 2, 3)]
    parts = [shift(parts[s - 1], "x", s) for s in (1, 2, 3)]
    bias = bias + shift(bias, "dp", 1)
    biases = [bias] + [shift(bias, "x", s) for s in (1, 2, 3)]
    wide = ((ROWS, HEADS * GROUP * HD), bf16)
    p_out, r_out, p_dq, r_dq = call(functools.partial(gather_heads_body, 1), 4, [wide] * 4, us=2)(
        sc, *back
    )
    p_own, r_own, p_far, bias = call(
        along_x_body,
        9,
        [((512, HD), f32)] * 2 + [((528, HD), bf16), ((8, HD), f32)],
        scalars=False,
        anywhere=(0,),
        us=2,
    )(p_out, own, *parts, *biases)
    p_far = shift(p_far, "branch", 1)
    dkv = call(settle_body, 8, [((4 * ROWS + 16, HD), bf16)] * 4)(
        sc, p_own, r_own, p_far, bias, *tables
    )
    dkv = [dkv[0]] + [shift(dkv[t], "z", t) for t in (1, 2, 3)]
    narrow = ((ROWS, HEADS * HD), bf16)
    p_dk, p_dv, r_dk, r_dv, qsum, ksum, vsum = call(
        finish_body,
        4,
        [narrow] * 4 + [((1, HEADS * GROUP * HD), f32)] + [((1, HEADS * HD), f32)] * 2,
    )(sc, *dkv)
    return (
        p_out[None],
        r_out[None, None],
        p_dq[None],
        p_dk[None],
        p_dv[None],
        r_dq[None, None],
        r_dk[None, None],
        r_dv[None, None],
        qsum.reshape(-1),
        ksum.reshape(-1),
        vsum.reshape(-1),
    )


def solution(mesh):
    fine = Mesh(mesh.devices.reshape(2, 4, 4, 2, 2), ("dp", "z", "x", "core", "branch"))
    prompt = P("dp", ("z", "x", "core", "branch"), None)
    reply = P("dp", "branch", ("z", "x", "core"), None)
    return jax.shard_map(
        on_device,
        mesh=fine,
        in_specs=(prompt,) * 4
        + (reply,) * 4
        + (P(),) * 3
        + (P("dp", ("z", "x", "core", "branch")), P("dp", "branch")),
        out_specs=(prompt, reply, prompt, prompt, prompt, reply, reply, reply, P(), P(), P()),
        check_vma=False,
    )
```

```python
import functools

import jax
import jax.numpy as jnp
import numpy as np
from jax import lax
from jax.experimental import pallas as pl
from jax.experimental.pallas import tpu as pltpu
from jax.sharding import Mesh
from jax.sharding import PartitionSpec as P

HEADS = 4
GROUP = 5
HD = 128
ROWS = 64
STRIPE = GROUP * ROWS
PROMPT = 4096
REPLY = 2048
BLOCK = 512
SCALE = HD**-0.5
LOG2 = float(SCALE * np.log2(np.e))
LOW = -1e30
MASKED = -3e38
KV = 2 * ROWS
PKV = KV + 16
OWN = PKV + KV
PIECE = 4 * OWN + 4 * PKV
TERMS = 1536

bf16 = jnp.bfloat16
f32 = jnp.float32
NT = (((1,), (1,)), ((), ()))
NN = (((1,), (0,)), ((), ()))
TN = (((0,), (0,)), ((), ()))


def dot(a, b, dims):
    return lax.dot_general(a, b, dims, preferred_element_type=f32)


def angle_tables():
    frequency = 1000000.0 ** (-(np.arange(HD // 2) * 2.0 / HD))
    frequency = np.concatenate([frequency, frequency])
    sign = np.where(np.arange(HD) < HD // 2, -1.0, 1.0)
    coarse = np.arange((PROMPT + REPLY) // ROWS)[:, None] * ROWS * frequency
    fine = np.arange(ROWS)[:, None] * frequency
    return [
        jnp.asarray(t.astype(np.float32))
        for t in (np.cos(coarse), np.sin(coarse) * sign, np.cos(fine), np.sin(fine) * sign)
    ]


def turn(tables, block):
    coarse_cos, coarse_sin, fine_cos, fine_sin = tables
    ca, sa = coarse_cos[pl.ds(block, 1), :], coarse_sin[pl.ds(block, 1), :]
    cb, sb = fine_cos[...], fine_sin[...]
    return ca * cb - sa * sb, sa * cb + ca * sb


def rotate(x, cosine, sine):
    return x * cosine + pltpu.roll(x, HD // 2, 1) * sine


def unrotate(x, cosine, sine):
    return x * cosine - pltpu.roll(x, HD // 2, 1) * sine


def prompt_block(sc, z):
    return z * 16 + sc[1] * 4 + sc[2] * 2 + sc[3]


def reply_block(sc, z):
    return z * 8 + sc[1] * 2 + sc[2]


def part(i):
    return pl.ds(pl.multiple_of(i, ROWS), ROWS)


def lanes(i):
    return pl.ds(pl.multiple_of(i * HD, HD), HD)


def prepare_kv_body(sc, pk, pv, rk, rv, bias, seg, t0, t1, t2, t3, *outs):
    tables = (t0, t1, t2, t3)
    z = sc[0]
    prompt_turn = turn(tables, prompt_block(sc, z))
    reply_turn = turn(tables, PROMPT // ROWS + reply_block(sc, z))
    ids = jnp.concatenate([seg[...], seg[...]], axis=1)
    row = lax.broadcasted_iota(jnp.int32, (16, HD), 0)
    lane = lax.broadcasted_iota(jnp.int32, (16, HD), 1)
    note = jnp.zeros((16, HD), f32)
    for s in range(1, HEADS):
        below = jnp.sum((ids < s).astype(f32), axis=1, keepdims=True) * 0.5
        note = jnp.where((row == 0) & (lane == s), below, note)
    note = jnp.where(row == 1, ids.astype(f32), note).astype(bf16)
    for s, out in enumerate(outs):
        h = lax.rem(z + s, HEADS)
        at = lanes(h)
        kb, vb = bias[pl.ds(20 + h, 1), :], bias[pl.ds(24 + h, 1), :]
        out[0:64, :] = rotate(pk[:, at].astype(f32) + kb, *prompt_turn).astype(bf16)
        out[64:128, :] = (pv[:, at].astype(f32) + vb).astype(bf16)
        out[128:144, :] = note
        out[144:208, :] = rotate(rk[:, at].astype(f32) + kb, *reply_turn).astype(bf16)
        out[208:272, :] = (rv[:, at].astype(f32) + vb).astype(bf16)


def prepare_q_body(sc, pq, pg, rq, rg, bias, t0, t1, t2, t3, *outs):
    tables = (t0, t1, t2, t3)
    z = sc[0]
    prompt_turn = turn(tables, prompt_block(sc, z))
    reply_turn = turn(tables, PROMPT // ROWS + reply_block(sc, z))
    place = reply_block(sc, z) * ROWS + lax.broadcasted_iota(jnp.int32, (ROWS, HD), 0)
    valid = place < sc[4]
    for s, out in enumerate(outs):
        h = lax.rem(z + s, HEADS) * GROUP
        for m in range(GROUP):
            at = lanes(h + m)
            qb = bias[pl.ds(h + m, 1), :]
            o = m * ROWS
            out[o : o + 64, :] = rotate(pq[:, at].astype(f32) + qb, *prompt_turn).astype(bf16)
            o += STRIPE
            out[o : o + 64, :] = pg[:, at]
            o += STRIPE
            out[o : o + 64, :] = rotate(rq[:, at].astype(f32) + qb, *reply_turn).astype(bf16)
            o += STRIPE
            out[o : o + 64, :] = jnp.where(valid, rg[:, at].astype(f32), 0.0).astype(bf16)


def granule(s, zz, sub=0):
    return s * 1024 + zz * 256 + sub * ROWS


def x_of(sc, s):
    return lax.rem(sc[1] + 4 - s, 4)


def prompt_rows(sc, i):
    pair = [granule(lax.rem(sc[1] + 4 - lax.rem(i, 2) * 2 - n, 4), i // 2) for n in range(2)]
    return [pl.ds(pl.multiple_of(row, 256), 256) for row in pair]


def prompt_block_of(sc, i, there, pk, pv, start, place):
    rows = prompt_rows(sc, i)
    key = lax.broadcasted_iota(jnp.int32, (BLOCK, STRIPE), 0)
    start, place = start - i * BLOCK, jnp.where(there, place - i * BLOCK, -1)
    k, v = [jnp.concatenate([ref[at, :] for at in rows], axis=0) for ref in (pk, pv)]
    return k, v, (key >= start) & (key <= place)


def prompt_limits(sc, j, start):
    lane = lax.broadcasted_iota(jnp.int32, start.shape, 1)
    first = jnp.sum(jnp.where(lane == 0, start, 0))
    return first // BLOCK, (prompt_block(sc, j) * ROWS + ROWS - 1) // BLOCK + 1


def reply_places(sc):
    column = lax.broadcasted_iota(jnp.int32, (1, 4 * STRIPE), 1)
    stripe = sum((column >= j * STRIPE).astype(jnp.int32) for j in range(1, 4))
    return reply_block(sc, stripe) * ROWS + jnp.bitwise_and(column, ROWS - 1)


def reply_seen(sc, key_at, place):
    key = lax.broadcasted_iota(jnp.int32, (BLOCK, place.shape[1]), 0)
    return key <= jnp.minimum(place, sc[4] - 1) - key_at


def prompt_places(sc, j):
    lane = lax.broadcasted_iota(jnp.int32, (1, STRIPE), 1)
    return prompt_block(sc, j) * ROWS + jnp.bitwise_and(lane, ROWS - 1)


def online(state, q, k, v, seen):
    top, total, acc = state
    scores = dot(k, q, NT) * LOG2
    if seen is not None:
        scores = jnp.where(seen, scores, MASKED)
    raised = jnp.maximum(top, jnp.max(scores, axis=0, keepdims=True))
    shrink = jnp.exp2(top - raised)
    p = jnp.exp2(scores - raised)
    total = total * shrink + jnp.sum(p, axis=0, keepdims=True)
    return raised, total, acc * shrink + dot(v, p.astype(bf16), TN)


def empty(n):
    return jnp.full((1, n), LOW, f32), jnp.zeros((1, n), f32), jnp.zeros((HD, n), f32)


def grads(q, g, lse, rd, k, v, seen):
    w = jnp.exp2(dot(k, q, NT) * LOG2 - lse)
    if seen is not None:
        w = jnp.where(seen, w, 0.0)
    ds = (w * (dot(v, g, NT) - rd)).astype(bf16)
    return dot(ds, q, NN), dot(w.astype(bf16), g, NN), dot(ds, k, TN)


def attend_body(sc, *refs):
    q_in, kv_in, tables = refs[0:4], refs[4:12], refs[12:16]
    back, keep, send = refs[16:20], refs[20], refs[21]
    (pq, pg, rq, rg, pk, pv, rk, rv, r_stat, p_stat, pdq, rdq, pdk, pdv, rdk, rdv,
     stat_m, stat_l, acc_r, p_out, r_out, note, bias, seen_from) = refs[22:46]
    p_top, p_total, p_acc = refs[46:48], refs[48:50], refs[50:52]
    z, x, core, b, length = sc[0], sc[1], sc[2], sc[3], sc[4]

    for s in range(4):
        at = pl.ds(pl.multiple_of(lax.rem(z + 4 - s, 4) * STRIPE, STRIPE), STRIPE)
        for i, ref in enumerate((pq, pg, rq, rg)):
            ref[at, :] = q_in[s][i * STRIPE : (i + 1) * STRIPE, :]
    counts = jnp.zeros((16, HD), f32)
    for s in range(4):
        xx = x_of(sc, s)
        for other in range(2):
            piece = kv_in[s * 2 + other]
            cc = core if other == 0 else 1 - core
            for t in range(4):
                zz = lax.rem(z + 4 - t, 4)
                to = part((zz * 8 + xx * 2 + cc) * ROWS)
                o = t * OWN + PKV
                rk[to, :] = piece[o : o + 64, :]
                rv[to, :] = piece[o + 64 : o + 128, :]
                for far in range(2):
                    bb = b if far == 0 else 1 - b
                    to = part(granule(s, zz, cc * 2 + bb))
                    o = t * OWN if far == 0 else 4 * OWN + t * PKV
                    pk[to, :] = piece[o : o + 64, :]
                    pv[to, :] = piece[o + 64 : o + 128, :]
                    told = piece[o + 128 : o + 144, :].astype(f32)
                    counts = counts + told
                    if s == 0 and other == 0 and far == 0:
                        note[pl.ds(zz, 1)] = told[None]

    lane = lax.broadcasted_iota(jnp.int32, (1, HD), 1)
    starts = [
        jnp.sum(jnp.where(lane == s, counts[0:1, :], 0.0)).astype(jnp.int32) for s in range(HEADS)
    ]

    reply_place = reply_places(sc)
    q_all = rq[...]

    def forward_reply(i, state):
        at = pl.ds(pl.multiple_of(i * 2 * BLOCK, 2 * BLOCK), 2 * BLOCK)
        return online(state, q_all, pk[at, :], pv[at, :], None)

    top, total, acc = lax.fori_loop(0, PROMPT // BLOCK // 2, forward_reply, empty(4 * STRIPE), unroll=2)
    half = 2 * STRIPE
    for i in range(4):
        at = slice(i * BLOCK, (i + 1) * BLOCK)
        if i < 2:
            seen = reply_seen(sc, i * BLOCK, reply_place)
            top, total, acc = online((top, total, acc), q_all, rk[at, :], rv[at, :], seen)
            if i == 1:
                stat_m[0:1, :] = top
                stat_l[0:1, :] = total
                acc_r[...] = acc
                state = (top[:, half:], total[:, half:], acc[:, half:])
        else:
            seen = reply_seen(sc, i * BLOCK, reply_place[:, half:])
            state = online(state, rq[half:, :], rk[at, :], rv[at, :], seen)
    stat_m[0:1, half:] = state[0]
    stat_l[0:1, half:] = state[1]
    acc_r[:, half:] = state[2]
    total = stat_l[0:1, :]
    out = jnp.where(reply_place < length, acc_r[...] / total, 0.0).astype(bf16).astype(f32)
    r_stat[0:1, :] = stat_m[0:1, :] + jnp.log2(total)
    r_stat[1:2, :] = jnp.sum(out * rg[...].astype(f32).T, axis=0, keepdims=True)
    acc_r[...] = out
    r_out[...] = acc_r[...].T

    lows, ends, total_blocks = [], [], 0
    for j in range(4):
        ids = note[j, 1:2, :].astype(jnp.int32)
        start = jnp.zeros((1, HD), jnp.int32)
        for s in range(1, HEADS):
            start = jnp.where(ids == s, starts[s], start)
        low, high = prompt_limits(sc, j, start)
        lows.append(low)
        total_blocks = total_blocks + high - low
        ends.append(total_blocks)
        seen_from[j, 0:1, :] = jnp.concatenate([start, start, start[:, :64]], axis=1)
    half_list = (total_blocks + 1) // 2

    def listed(i, side):
        n = i + side * half_list
        j, low, before = 0, lows[0], 0
        for k in range(3):
            later = n >= ends[k]
            j = jnp.where(later, k + 1, j)
            low = jnp.where(later, lows[k + 1], low)
            before = jnp.where(later, ends[k], before)
        there = n < total_blocks
        return j, jnp.where(there, low + n - before, 0), there

    def stripe_rows(j):
        return pl.ds(pl.multiple_of(j * STRIPE, STRIPE), STRIPE)

    def seen_block(j, block, there):
        return prompt_block_of(
            sc, block, there, pk, pv, seen_from[j, 0:1, :], prompt_places(sc, j)
        )

    for side in range(2):
        p_top[side][...] = jnp.full_like(p_top[side], LOW)
        p_total[side][...] = jnp.zeros_like(p_total[side])
        p_acc[side][...] = jnp.zeros_like(p_acc[side])

    def forward_prompt(i, carry):
        for side in range(2):
            j, block, there = listed(i, side)
            k, v, seen = seen_block(j, block, there)
            state = p_top[side][j, 0:1, :], p_total[side][j, 0:1, :], p_acc[side][j]
            top, total, acc = online(state, pq[stripe_rows(j), :], k, v, seen)
            p_top[side][j, 0:1, :] = top
            p_total[side][j, 0:1, :] = total
            p_acc[side][j] = acc
        return carry

    lax.fori_loop(0, half_list, forward_prompt, 0)
    for j in range(4):
        rows = slice(j * STRIPE, (j + 1) * STRIPE)
        tops = [p_top[side][j, 0:1, :] for side in range(2)]
        top = jnp.maximum(*tops)
        shrinks = [jnp.exp2(t - top) for t in tops]
        total = sum(p_total[side][j, 0:1, :] * shrinks[side] for side in range(2))
        acc = sum(p_acc[side][j] * shrinks[side] for side in range(2))
        out = (acc / total).astype(bf16).astype(f32)
        p_stat[j, 0:1, :] = top + jnp.log2(total)
        p_stat[j, 1:2, :] = jnp.sum(out * pg[rows, :].astype(f32).T, axis=0, keepdims=True)
        p_out[rows, :] = out.T
    for s in range(4):
        at = pl.ds(pl.multiple_of(lax.rem(z + 4 - s, 4) * STRIPE, STRIPE), STRIPE)
        back[s][0:STRIPE, :] = p_out[at, :].astype(bf16)
        back[s][STRIPE : 2 * STRIPE, :] = r_out[at, :].astype(bf16)

    pdq[...] = jnp.zeros_like(pdq)
    rdq[...] = jnp.zeros_like(rdq)
    bias[...] = jnp.zeros_like(bias)

    def backward_reply(i, carry):
        at = pl.ds(pl.multiple_of(i * BLOCK, BLOCK), BLOCK)
        dk, dv, dq = grads(
            rq[...], rg[...], r_stat[0:1, :], r_stat[1:2, :], pk[at, :], pv[at, :], None
        )
        pdk[at, :] = dk
        pdv[at, :] = dv
        rdq[...] += dq
        return carry

    lax.fori_loop(0, PROMPT // BLOCK, backward_reply, 0, unroll=2)

    def backward_prompt(i, carry):
        done = []
        for side in range(2):
            j, block, there = listed(i, side)
            k, v, seen = seen_block(j, block, there)
            rows = stripe_rows(j)
            terms = grads(
                pq[rows, :], pg[rows, :], p_stat[j, 0:1, :], p_stat[j, 1:2, :], k, v, seen
            )
            done.append((rows, prompt_rows(sc, block), terms))
        for rows, keys, (dk, dv, dq) in done:
            for n, at in enumerate(keys):
                pdk[at, :] += dk[n * 256 : (n + 1) * 256, :]
                pdv[at, :] += dv[n * 256 : (n + 1) * 256, :]
            pdq[rows, :] += dq
        return carry

    lax.fori_loop(0, half_list, backward_prompt, 0)
    for i in range(4):
        at = slice(i * BLOCK, (i + 1) * BLOCK)
        cols = slice(0 if i < 2 else half, 4 * STRIPE)
        dk, dv, dq = grads(
            rq[cols, :], rg[cols, :], r_stat[0:1, cols], r_stat[1:2, cols], rk[at, :], rv[at, :],
            reply_seen(sc, i * BLOCK, reply_place[:, cols]),
        )
        rdk[at, :] = dk
        rdv[at, :] = dv
        rdq[cols, :] += dq

    coarse_cos, coarse_sin, fine_cos, fine_sin = tables

    def add(keys, values, row, block, sums):
        key = keys[pl.ds(pl.multiple_of(row, 256), 256), :]
        value = values[pl.ds(pl.multiple_of(row, 256), 256), :]
        for i in range(4):
            cut = slice(i * ROWS, (i + 1) * ROWS)
            at = pl.ds(block + i, 1)
            sums = (
                sums[0] + key[cut] * coarse_cos[at, :],
                sums[1] + key[cut] * coarse_sin[at, :],
                sums[2] + value[cut],
            )
        return sums

    sums = (jnp.zeros((ROWS, HD), f32),) * 3
    for s in range(4):
        sums = lax.fori_loop(
            0, 4, lambda zz, c, s=s: add(pdk, pdv, granule(s, zz), zz * 16 + x_of(sc, s) * 4, c), sums
        )
    sums = lax.fori_loop(0, 8, lambda i, c: add(rdk, rdv, i * 256, PROMPT // ROWS + i * 4, c), sums)
    key_sum = unrotate(sums[0] + pltpu.roll(sums[1], HD // 2, 1), fine_cos[...], fine_sin[...])
    bias[5:6, :] = jnp.sum(key_sum, axis=0, keepdims=True) * SCALE
    bias[6:7, :] = jnp.sum(sums[2], axis=0, keepdims=True)
    for s in range(4):
        zz = lax.rem(z + 4 - s, 4)
        for i, (ref, block) in enumerate(
            ((pdq, prompt_block(sc, zz)), (rdq, PROMPT // ROWS + reply_block(sc, zz)))
        ):
            cosine, sine = turn(tables, block)
            for m in range(GROUP):
                at = part(zz * STRIPE + m * ROWS)
                pre = unrotate(ref[at, :] * SCALE, cosine, sine)
                bias[m : m + 1, :] += jnp.sum(pre, axis=0, keepdims=True)
                o = (2 + i) * STRIPE + m * ROWS
                back[s][o : o + ROWS, :] = pre.astype(bf16)

    for s in range(4):
        xx = lax.rem(x + s, 4)
        for t in range(4):
            zz = lax.rem(z + t, 4)
            for far in range(2):
                bb = b if far == 0 else 1 - b
                own = part(granule((4 - s) % 4, zz, core * 2 + bb))
                theirs = part(granule((4 - s) % 4, zz, (1 - core) * 2 + bb))
                o = s * TERMS + far * 512 + t * ROWS
                keep[o : o + 64, :] = (pdk[own, :] * SCALE).astype(bf16)
                keep[o + 256 : o + 320, :] = pdv[own, :].astype(bf16)
                send[o : o + 64, :] = (pdk[theirs, :] * SCALE).astype(bf16)
                send[o + 256 : o + 320, :] = pdv[theirs, :].astype(bf16)
            own = part((zz * 8 + xx * 2 + core) * ROWS)
            theirs = part((zz * 8 + xx * 2 + 1 - core) * ROWS)
            o = s * TERMS + 1024 + t * ROWS
            keep[o : o + 64, :] = (rdk[own, :] * SCALE).astype(bf16)
            keep[o + 256 : o + 320, :] = rdv[own, :].astype(bf16)
            send[o : o + 64, :] = (rdk[theirs, :] * SCALE).astype(bf16)
            send[o + 256 : o + 320, :] = rdv[theirs, :].astype(bf16)
    words = two_words(bias[...])
    keep[4 * TERMS :, :] = words
    send[4 * TERMS :, :] = words


def two_words(x):
    high = x.astype(bf16).astype(f32)
    return jnp.concatenate([high, x - high], axis=0).astype(bf16)


def one_word(x):
    x = x.astype(f32)
    return x[0:8] + x[8:16]


def along_core_body(keep, got, near, *parts):
    at = slice(4 * TERMS, 4 * TERMS + 16)
    words = two_words(one_word(keep[at, :]) + one_word(got[at, :]))
    for i, out in enumerate((near, *parts)):
        at = slice(i * TERMS, (i + 1) * TERMS)
        out[0:TERMS, :] = (keep[at, :].astype(f32) + got[at, :].astype(f32)).astype(out.dtype)
        out[TERMS : TERMS + 16, :] = words.astype(out.dtype)


def along_x_body(after, own, r1, r2, r3, p_own, r_own, p_far, bias):
    total = own[0:TERMS, :] + (
        r1[0:TERMS, :].astype(f32) + r2[0:TERMS, :].astype(f32) + r3[0:TERMS, :].astype(f32)
    )
    b0, b1, b2, b3 = [one_word(r[TERMS : TERMS + 16, :]) for r in (own, r1, r2, r3)]
    words = two_words((b0 + b2) + (b1 + b3))
    p_own[...] = total[0:512]
    r_own[...] = total[1024:1536]
    p_far[0:512, :] = total[512:1024].astype(bf16)
    p_far[512:528, :] = words
    bias[...] = one_word(words)


def settle_body(sc, p_own, r_own, p_far, b0, b2, b3, t0, t1, t2, t3, *outs):
    tables = (t0, t1, t2, t3)
    z = sc[0]
    words = two_words((b0[...] + one_word(p_far[512:528, :])) + (b2[...] + b3[...]))
    for t, out in enumerate(outs):
        zz = lax.rem(z + t, 4)
        o = t * ROWS
        key = p_own[o : o + 64, :] + p_far[o : o + 64, :].astype(f32)
        out[0:64, :] = unrotate(key, *turn(tables, prompt_block(sc, zz))).astype(bf16)
        value = p_own[o + 256 : o + 320, :] + p_far[o + 256 : o + 320, :].astype(f32)
        out[64:128, :] = value.astype(bf16)
        block = PROMPT // ROWS + reply_block(sc, zz)
        out[128:192, :] = unrotate(r_own[o : o + 64, :], *turn(tables, block)).astype(bf16)
        out[192:256, :] = r_own[o + 256 : o + 320, :].astype(bf16)
        out[256:272, :] = words


def finish_body(sc, *refs):
    pieces, outs, (qsum, ksum, vsum) = refs[0:4], refs[4:8], refs[8:]
    z = sc[0]
    for t, piece in enumerate(pieces):
        h = lax.rem(z + 4 - t, 4)
        for i, out in enumerate(outs):
            out[:, lanes(h)] = piece[i * ROWS : (i + 1) * ROWS, :]
        bias = one_word(piece[256:272, :])
        for m in range(GROUP):
            qsum[:, lanes(h * GROUP + m)] = bias[m : m + 1]
        ksum[:, lanes(h)] = bias[5:6]
        vsum[:, lanes(h)] = bias[6:7]


def gather_heads_body(step, sc, *refs):
    pieces, outs = refs[:4], refs[4:]
    z = sc[0]
    for s, piece in enumerate(pieces):
        h = lax.rem(z + (s * step) % 4, 4)
        width = piece.shape[0] // ROWS // len(outs)
        for i, out in enumerate(outs):
            for m in range(width):
                o = (i * width + m) * ROWS
                out[:, lanes(h * width + m)] = piece[o : o + ROWS, :]


def call(body, n_in, outs, scratch=(), scalars=True, anywhere=(), us=1, mib=16):
    spec = pl.BlockSpec(memory_space=pltpu.VMEM)
    first = [pl.BlockSpec(memory_space=pltpu.SMEM)] if scalars else []
    ins = [pl.BlockSpec(memory_space=pl.ANY) if i in anywhere else spec for i in range(n_in)]
    return pl.pallas_call(
        body,
        in_specs=first + ins,
        out_specs=[spec] * len(outs),
        out_shape=[jax.ShapeDtypeStruct(s, t) for s, t in outs],
        scratch_shapes=list(scratch),
        cost_estimate=pl.CostEstimate(
            flops=us * 1000000, bytes_accessed=us * 3000000, transcendentals=0
        ),
        compiler_params=pltpu.CompilerParams(vmem_limit_bytes=mib * 1024 * 1024),
    )


def shift(v, axis, s):
    n = lax.axis_size(axis)
    return lax.ppermute(v, axis, [(i, (i + s) % n) for i in range(n)])


def on_device(pq, pk, pv, pg, rq, rk, rv, rg, qbias, kbias, vbias, segments, lengths):
    sc = jnp.stack(
        [lax.axis_index(a) for a in ("z", "x", "core", "branch")] + [lengths[0, 0]]
    ).astype(jnp.int32)
    tables = angle_tables()
    bias = jnp.concatenate([qbias, kbias, vbias]).astype(f32).reshape(-1, HD)
    kv = call(prepare_kv_body, 10, [((OWN, HD), bf16)] * 4, mib=56)(
        sc, pk[0], pv[0], rk[0, 0], rv[0, 0], bias, segments, *tables
    )
    q = call(prepare_q_body, 9, [((4 * STRIPE, HD), bf16)] * 4, mib=56)(
        sc, pq[0], pg[0], rq[0, 0], rg[0, 0], bias, *tables
    )
    kv = jnp.stack([kv[0]] + [shift(kv[s], "z", s) for s in (1, 2, 3)])
    kv, q = lax.optimization_barrier((kv, q))
    q = [q[0]] + [shift(q[s], "z", s) for s in (1, 2, 3)]
    far = shift(kv[:, :PKV].reshape(4 * PKV, HD), "branch", 1)
    kv = jnp.concatenate([kv.reshape(4 * OWN, HD), far])
    across = [kv] + [shift(kv, "x", s) for s in (1, 2, 3)]
    across[2], q = lax.optimization_barrier((across[2], q))
    pieces = [v for piece in across for v in (piece, shift(piece, "core", 1))]

    rows = 4 * STRIPE
    outs = call(
        attend_body,
        16,
        [((rows, HD), bf16)] * 4 + [((4 * TERMS + 16, HD), bf16)] * 2,
        [pltpu.VMEM((rows, HD), bf16)] * 4
        + [pltpu.VMEM((PROMPT, HD), bf16)] * 2
        + [pltpu.VMEM((REPLY, HD), bf16)] * 2
        + [pltpu.VMEM((8, rows), f32), pltpu.VMEM((4, 8, STRIPE), f32)]
        + [pltpu.VMEM((rows, HD), f32)] * 2
        + [pltpu.VMEM((PROMPT, HD), f32)] * 2
        + [pltpu.VMEM((REPLY, HD), f32)] * 2
        + [pltpu.VMEM((8, rows), f32)] * 2
        + [pltpu.VMEM((HD, rows), f32)]
        + [pltpu.VMEM((rows, HD), f32)] * 2
        + [pltpu.VMEM((4, 16, HD), f32), pltpu.VMEM((8, HD), f32)]
        + [pltpu.VMEM((4, 8, STRIPE), jnp.int32)]
        + [pltpu.VMEM((4, 8, STRIPE), f32)] * 4
        + [pltpu.VMEM((4, HD, STRIPE), f32)] * 2,
        us=60,
        mib=40,
    )(sc, *q, *pieces, *tables)
    back, (keep, send) = outs[:4], outs[4:]
    own, *parts = call(
        along_core_body,
        2,
        [((TERMS + 16, HD), f32)] + [((TERMS + 16, HD), bf16)] * 3,
        scalars=False,
        us=2,
    )(keep, shift(send, "core", 1))
    back = [back[0]] + [shift(back[s], "z", -s) for s in (1, 2, 3)]
    parts = [shift(parts[s - 1], "x", s) for s in (1, 2, 3)]
    wide = ((ROWS, HEADS * GROUP * HD), bf16)
    p_out, r_out, p_dq, r_dq = call(functools.partial(gather_heads_body, 1), 4, [wide] * 4, us=2)(
        sc, *back
    )
    p_own, r_own, p_far, bias = call(
        along_x_body,
        5,
        [((512, HD), f32)] * 2 + [((528, HD), bf16), ((8, HD), f32)],
        scalars=False,
        anywhere=(0,),
        us=2,
    )(p_out, own, *parts)
    p_far = shift(p_far, "branch", 1)
    across = lax.ppermute(bias, ("dp", "branch"), [(0, 3), (1, 2), (2, 1), (3, 0)])
    dkv = call(settle_body, 10, [((4 * ROWS + 16, HD), bf16)] * 4)(
        sc, p_own, r_own, p_far, bias, shift(bias, "dp", 1), across, *tables
    )
    dkv = [dkv[0]] + [shift(dkv[t], "z", t) for t in (1, 2, 3)]
    narrow = ((ROWS, HEADS * HD), bf16)
    p_dk, p_dv, r_dk, r_dv, qsum, ksum, vsum = call(
        finish_body,
        4,
        [narrow] * 4 + [((1, HEADS * GROUP * HD), f32)] + [((1, HEADS * HD), f32)] * 2,
    )(sc, *dkv)
    return (
        p_out[None],
        r_out[None, None],
        p_dq[None],
        p_dk[None],
        p_dv[None],
        r_dq[None, None],
        r_dk[None, None],
        r_dv[None, None],
        qsum.reshape(-1),
        ksum.reshape(-1),
        vsum.reshape(-1),
    )


def solution(mesh):
    fine = Mesh(mesh.devices.reshape(2, 4, 4, 2, 2), ("dp", "z", "x", "core", "branch"))
    prompt = P("dp", ("z", "x", "core", "branch"), None)
    reply = P("dp", "branch", ("z", "x", "core"), None)
    return jax.shard_map(
        on_device,
        mesh=fine,
        in_specs=(prompt,) * 4
        + (reply,) * 4
        + (P(),) * 3
        + (P("dp", ("z", "x", "core", "branch")), P("dp", "branch")),
        out_specs=(prompt, reply, prompt, prompt, prompt, reply, reply, reply, P(), P(), P()),
        check_vma=False,
    )
```
